128 devices in a mesh: dp: 32 (over x, z, core), tensor: 4 (over y).
Axes of the slice: x: 4, y: 4, z: 4, core: 2. Of those that a mesh axis runs over, the one named last changes fastest.
Arguments:
- hidden: bfloat16 [8192, 2048], P('dp'), may hold values from -200 to 200
- norm_gain: float32 [2048], replicated, may hold values from 0.5 to 2
- expert_ids: int32 [8192, 8], P(('dp', 'tensor')), may hold values from 0 to 127, all different within a row; in each aligned block of 64 rows (0 to 63, 64 to 127, ...) at most 8 rows name the same one
- gate_probs: float32 [8192, 8], P(('dp', 'tensor')), may hold values from 0.05 to 0.5
- out_grad: bfloat16 [8192, 2048], P(('dp', 'tensor')), may hold values from -8 to 8
- gate_weight: bfloat16 [128, 2048, 768], P(('dp', 'tensor')), may hold values from -0.125 to 0.125
- up_weight: bfloat16 [128, 2048, 768], P(('dp', 'tensor')), may hold values from -0.125 to 0.125
- down_weight: bfloat16 [128, 768, 2048], P(('dp', 'tensor')), may hold values from -0.21875 to 0.21875
Outputs:
- layer_out: bfloat16 [8192, 2048], P(('dp', 'tensor'))
- input_grad: bfloat16 [8192, 2048], P('dp')
- gate_grad: float32 [8192, 8], P(('dp', 'tensor'))
- gain_grad: float32 [2048], replicated
- gate_weight_grad: bfloat16 [128, 2048, 768], P(('dp', 'tensor'))
- up_weight_grad: bfloat16 [128, 2048, 768], P(('dp', 'tensor'))
- down_weight_grad: bfloat16 [128, 768, 2048], P(('dp', 'tensor'))
The draws below stay inside these ranges and needn't reach their ends.
Inputs may be any that keep to these rules, and one draw needn't show every extreme that they name: `expert_ids`: within the rows of one device no expert is named by more than 8 rows, a bound that some block reaches.
All inputs are finite; a program needn't handle non-finite values.
Results may differ from the reference program's by a relative error of at most 0.0072.
Values may be sent and summed in bfloat16 or wider, within the bound.
No kernel may reach another device: no remote copies, remote signals or barrier semaphores. Data moves between devices by JAX's collectives and lax.ppermute only.
A program may use at most 128 MiB of HBM per device.

```python
import math
import jax
import jax.numpy as jnp
import numpy as np
from jax import lax

D = 2048
FF = 768
TOPK = 8
EXPERTS = 128
TOKENS = 8192
ROWS_DEV = 64
CAP = 8
SLOTS = 1024


def draw_hidden(key, part):
    first, second, third = jax.random.split(key, 3)
    row_scale = jnp.exp(jax.random.uniform(first, (TOKENS, 1), jnp.float32, 0.0, math.log(10.0)))
    col_scale = jnp.exp(jax.random.uniform(second, (1, D), jnp.float32, 0.0, math.log(10.0)))
    base = jnp.clip(jax.random.normal(third, (TOKENS, D), jnp.float32), -6.0, 6.0)
    return (0.3 * base * row_scale * col_scale).astype(jnp.bfloat16)


def draw_out_grad(key, part):
    first = jax.random.fold_in(key, 0)
    ramp = jnp.arange(TOKENS, dtype=jnp.float32)[:, None] / float(max(TOKENS - 1, 1))
    rising = jnp.exp(math.log(3.0) * ramp)
    base = jnp.clip(jax.random.normal(first, (TOKENS, D), jnp.float32), -6.0, 6.0)
    return (0.3 * base * rising).astype(jnp.bfloat16)


def block_scale(own_key, dims, cuts, smallest, top_value):
    def one(dim, parts):
        steps = jax.random.uniform(jax.random.fold_in(jax.random.fold_in(own_key, 6), dim), (parts,), jnp.float32, smallest / len(cuts), top_value / len(cuts))
        return jnp.repeat(jnp.exp(steps), dims[dim] // parts).reshape((-1,) + (1,) * (len(dims) - dim - 1))

    gain = one(*cuts[0])
    for cut in cuts[1:]:
        gain = gain * one(*cut)
    return gain


def shared_out(own_key, own, number, rows, number_of, top, limit, lean):
    ranking = jax.random.permutation(own_key, number_of)
    heavy_load, usual = portions_of(number_of, rows * top, limit, lean, True), portions_of(number_of, rows * top, limit, lean, False)
    places = jnp.arange(number_of)

    def named(tallies, offset_by):
        used = int((tallies > 0).sum())
        fixed = max(1, used // 4)
        passed = fixed + (places - fixed + offset_by * (used - fixed)) % max(1, number_of - fixed)
        return jnp.zeros((number_of,), jnp.int32).at[ranking[jnp.where(places < fixed, places, passed)]].set(jnp.asarray(tallies, jnp.int32))

    tallies = jnp.where(number % 4 == 0, named(heavy_load, number // 4), named(usual, number - number // 4 - 1))
    mixed = jax.random.permutation(jax.random.fold_in(own, 3), number_of)
    source_of, receiver = mixed[0:number_of // 2 * 2:2], mixed[1:number_of // 2 * 2:2]
    slack = jnp.minimum(tallies[source_of] - 1, limit - tallies[receiver]) // 2
    slack = jnp.where((source_of == ranking[0]) | (receiver == ranking[0]) | (tallies[receiver] == 0), 0, jnp.maximum(slack, 0))
    passed = jax.random.randint(jax.random.fold_in(own, 4), (number_of // 2,), 0, 1 << 20) % (slack + 1)
    tallies = tallies.at[source_of].add(-passed).at[receiver].add(passed)
    labels = jnp.searchsorted(jnp.cumsum(tallies), jnp.arange(rows * top), side="right").astype(jnp.int32)
    listing = labels.reshape(top, rows).T
    listing = listing[jax.random.permutation(jax.random.fold_in(own, 1), rows)]
    offset_by = jax.random.randint(jax.random.fold_in(own, 2), (rows, 1), 0, top)
    return jnp.take_along_axis(listing, (jnp.arange(top)[None, :] + offset_by) % top, axis=1)


def portions_of(amount, total, reach, lean, full):
    portions = [(1 << 20) // math.isqrt(grade ** lean) + 1 for grade in range(1, amount + 1)]
    largest = reach if full else min(reach, max(-(-total // amount), total * portions[0] // sum(portions)))
    least = 1 if total - largest >= amount - 1 else 0
    counts, surplus = [largest] + [least] * (amount - 1), total - largest - least * (amount - 1)
    while surplus > 0:
        free = [i for i in range(1, amount) if counts[i] < largest] or [i for i in range(1, amount) if counts[i] < reach]
        whole, remaining = sum([portions[i] for i in free]), surplus
        for i in free:
            more = min(reach - counts[i], max(1, remaining * portions[i] // whole), surplus)
            counts[i] = counts[i] + more
            surplus = surplus - more
    return np.array(counts)


def scatter_about(key, extent, width, most, shards=(), kind=jnp.bfloat16):
    values = width * jax.random.normal(key, extent, jnp.float32)
    if shards:
        values = values * block_scale(key, extent, shards, -0.22, 0.18)
    return jnp.clip(values, -most, most).astype(kind)


def setup_inputs(seed: int = 0) -> dict:
    key_list = jax.random.split(jax.random.key(seed), 9)
    hidden = draw_hidden(jax.random.fold_in(key_list[8], 71), 0)
    norm_gain = jnp.clip(jnp.exp(jax.random.uniform(key_list[1], (D,), jnp.float32, math.log(0.5), math.log(2.0))), 0.5, 2.0)
    expert_ids_keys = jax.random.split(jax.random.fold_in(key_list[2], 1), TOKENS // ROWS_DEV)
    expert_ids_turns = jax.random.permutation(jax.random.fold_in(key_list[2], 3), TOKENS // ROWS_DEV)
    expert_ids = jax.vmap(lambda own, number: shared_out(jax.random.fold_in(key_list[2], 2), own, number, ROWS_DEV, EXPERTS, TOPK, CAP, 2))(expert_ids_keys, expert_ids_turns).reshape((TOKENS, TOPK))
    gate_probs = jnp.clip(jnp.exp(math.log(0.5) - 2.3025851 * jax.random.uniform(key_list[3], (TOKENS, TOPK), jnp.float32) ** block_scale(key_list[3], (TOKENS, TOPK), ((0, 128),), -0.2, 0.2)), 0.05, 0.5)
    out_grad = draw_out_grad(jax.random.fold_in(key_list[8], 71), 0)
    gate_weight = scatter_about(key_list[5], (EXPERTS, D, FF), D ** -0.5, 0.125, ((0, 128),))
    up_weight = scatter_about(key_list[6], (EXPERTS, D, FF), D ** -0.5, 0.125, ((0, 128),))
    down_weight = scatter_about(key_list[7], (EXPERTS, FF, D), FF ** -0.5, 0.21875, ((0, 128),))
    return {"hidden": hidden, "norm_gain": norm_gain, "expert_ids": expert_ids, "gate_probs": gate_probs, "out_grad": out_grad, "gate_weight": gate_weight, "up_weight": up_weight, "down_weight": down_weight}


epsilon = 1e-06

def reference(hidden, norm_gain, expert_ids, gate_probs, out_grad, gate_weight, up_weight, down_weight):
    values = hidden.astype(jnp.float32)
    inverse = lax.rsqrt(lax.optimization_barrier(jnp.mean(values * values, axis=-1, keepdims=True)) + epsilon)
    unit_rows = values * inverse
    normed = (unit_rows * norm_gain).astype(jnp.bfloat16)
    grad_rows = out_grad.astype(jnp.float32)
    scaled = (gate_probs[:, :, None] * grad_rows[:, None, :]).astype(jnp.bfloat16)
    total_pairs = TOKENS * TOPK
    flat_ids = expert_ids.reshape(-1).astype(jnp.int32)
    normed_pad = jnp.concatenate([normed, jnp.zeros((1, D), jnp.bfloat16)], axis=0)
    scaled_pad = jnp.concatenate([scaled.reshape(total_pairs, D), jnp.zeros((1, D), jnp.bfloat16)], axis=0)

    def single(operands):
        expert, w_gate, w_up, w_down = operands
        found = jnp.nonzero(flat_ids == expert, size=SLOTS, fill_value=total_pairs)[0].astype(jnp.int32)
        token = jnp.where(found < total_pairs, found // TOPK, TOKENS).astype(jnp.int32)
        inputs = normed_pad[token]
        cotan = scaled_pad[found]
        gate_pre = jnp.dot(inputs, w_gate, preferred_element_type=jnp.float32)
        up_pre = jnp.dot(inputs, w_up, preferred_element_type=jnp.float32)
        sigma = jax.nn.sigmoid(gate_pre)
        silu_vals = gate_pre * sigma
        act = (silu_vals * up_pre).astype(jnp.bfloat16)
        result = jnp.dot(act, w_down, preferred_element_type=jnp.float32).astype(jnp.bfloat16)
        act_grad = jnp.dot(cotan, w_down.T, preferred_element_type=jnp.float32)
        gate_pgrad = (act_grad * up_pre * sigma * (1.0 + gate_pre * (1.0 - sigma))).astype(jnp.bfloat16)
        up_pgrad = (act_grad * silu_vals).astype(jnp.bfloat16)
        down_g = jnp.dot(act.T, cotan, preferred_element_type=jnp.float32).astype(jnp.bfloat16)
        gate_g = jnp.dot(inputs.T, gate_pgrad, preferred_element_type=jnp.float32).astype(jnp.bfloat16)
        up_g = jnp.dot(inputs.T, up_pgrad, preferred_element_type=jnp.float32).astype(jnp.bfloat16)
        back = jnp.dot(gate_pgrad, w_gate.T, preferred_element_type=jnp.float32)
        back = back + jnp.dot(up_pgrad, w_up.T, preferred_element_type=jnp.float32)
        return (result, back.astype(jnp.bfloat16), found, gate_g, up_g, down_g)
    numbers = jnp.arange(EXPERTS, dtype=jnp.int32)
    results, backs, founds, gate_g, up_g, down_g = lax.map(single, (numbers, gate_weight, up_weight, down_weight))
    where_all = founds.reshape(-1).astype(jnp.int32)
    out_rows = jnp.zeros((total_pairs + 1, D), jnp.bfloat16).at[where_all].set(results.reshape(-1, D))
    out_rows = out_rows[:total_pairs].reshape(TOKENS, TOPK, D)
    back_rows = jnp.zeros((total_pairs + 1, D), jnp.bfloat16).at[where_all].set(backs.reshape(-1, D))
    back_rows = back_rows[:total_pairs].reshape(TOKENS, TOPK, D)
    out_f = out_rows.astype(jnp.float32)
    layer_out = (values + lax.optimization_barrier(jnp.sum(gate_probs[:, :, None] * out_f, axis=1))).astype(jnp.bfloat16)
    gate_grad = lax.optimization_barrier(jnp.sum(grad_rows[:, None, :] * out_f, axis=2))
    normed_total = lax.optimization_barrier(jnp.sum(back_rows.astype(jnp.float32), axis=1))
    gain_grad = lax.optimization_barrier(jnp.sum(normed_total * unit_rows, axis=0))
    upstream = normed_total * norm_gain
    input_grad = grad_rows + inverse * (upstream - unit_rows * lax.optimization_barrier(jnp.mean(upstream * unit_rows, axis=-1, keepdims=True)))
    return (layer_out, input_grad.astype(jnp.bfloat16), gate_grad, gain_grad, gate_g, up_g, down_g)
```

```python
import jax
import jax.numpy as jnp
from jax import lax
from jax.experimental import pallas as pl
from jax.experimental.pallas import tpu as pltpu
from jax.sharding import PartitionSpec as P

epsilon = 1e-06
AXES = ("dp", "tensor")
BF16 = jnp.bfloat16
F32 = jnp.float32
VMEM_LIMIT = 48 * 1024 * 1024


def slot_rows(ids_t, first, count, cap):
    top, tokens = ids_t.shape
    names = lax.broadcasted_iota(jnp.int32, (count, tokens), 0) + first
    named = jnp.zeros((count, tokens), F32)
    for k in range(top):
        named = named + jnp.where(ids_t[k : k + 1, :] == names, 1.0, 0.0)
    before = jnp.where(
        lax.broadcasted_iota(jnp.int32, (tokens, tokens), 0)
        < lax.broadcasted_iota(jnp.int32, (tokens, tokens), 1),
        1.0,
        0.0,
    ).astype(BF16)
    rank = jnp.dot(named.astype(BF16), before, preferred_element_type=F32)
    rank = jnp.where(named > 0.0, rank, -1.0)
    place = lax.broadcasted_iota(jnp.int32, (count, cap, tokens), 1).astype(F32)
    return jnp.where(rank[:, None, :] == place, 1.0, 0.0)


def pack_normed_kernel(quarter, ids_t, hidden, gain, buf, normed):
    step = pl.program_id(0)
    rows, count, cap = buf.shape[0], buf.shape[0] // 8, 8

    @pl.when(step == 0)
    def _():
        values = hidden[...].astype(F32)
        inverse = lax.rsqrt(jnp.mean(values * values, axis=-1, keepdims=True) + epsilon)
        normed[...] = (values * inverse * gain[...]).astype(BF16)

    chosen = slot_rows(ids_t[...], step * count, count, cap).reshape(rows, -1).astype(BF16)
    buf[...] = jnp.dot(chosen, normed[...], preferred_element_type=F32).astype(BF16)


def pack_scaled_kernel(ids_t, probs_t, grad, buf):
    step = pl.program_id(0)
    rows, count, cap = buf.shape[0], buf.shape[0] // 8, 8
    ids = ids_t[...]
    top, tokens = ids.shape
    chosen = slot_rows(ids, step * count, count, cap)
    names = lax.broadcasted_iota(jnp.int32, (count, tokens), 0) + step * count
    prob = jnp.zeros((count, tokens), F32)
    for k in range(top):
        prob = prob + jnp.where(ids[k : k + 1, :] == names, probs_t[k : k + 1, :], 0.0)
    weight = jnp.sum((chosen * prob[:, None, :]).reshape(rows, tokens), axis=1, keepdims=True)
    picked = jnp.dot(
        chosen.reshape(rows, tokens).astype(BF16), grad[...], preferred_element_type=F32
    )
    buf[...] = (picked * weight).astype(BF16)


def routes_kernel(ids, probs, routes, weights):
    tokens, top = ids.shape
    slots = routes.shape[1]
    cap = 8
    experts = slots // cap
    names = lax.broadcasted_iota(jnp.int32, (tokens, experts), 1)
    named = jnp.zeros((tokens, experts), F32)
    prob = jnp.zeros((tokens, experts), F32)
    for k in range(top):
        hit = ids[:, k : k + 1] == names
        named = named + jnp.where(hit, 1.0, 0.0)
        prob = prob + jnp.where(hit, probs[:, k : k + 1], 0.0)
    before = jnp.where(
        lax.broadcasted_iota(jnp.int32, (tokens, tokens), 1)
        < lax.broadcasted_iota(jnp.int32, (tokens, tokens), 0),
        1.0,
        0.0,
    ).astype(BF16)
    rank = jnp.dot(before, named.astype(BF16), preferred_element_type=F32)
    rank = jnp.where(named > 0.0, rank, -1.0).astype(BF16)
    spread = jnp.where(
        lax.broadcasted_iota(jnp.int32, (experts, slots), 1) // cap
        == lax.broadcasted_iota(jnp.int32, (experts, slots), 0),
        1.0,
        0.0,
    ).astype(BF16)
    place = (lax.broadcasted_iota(jnp.int32, (tokens, slots), 1) % cap).astype(F32)
    chosen = jnp.where(
        jnp.dot(rank, spread, preferred_element_type=F32) == place, 1.0, 0.0
    )
    routes[...] = chosen.astype(BF16)
    left = prob
    for part in range(3):
        piece = left.astype(BF16)
        left = left - piece.astype(F32)
        weights[part * tokens : (part + 1) * tokens, :] = (
            chosen * jnp.dot(piece, spread, preferred_element_type=F32)
        ).astype(BF16)


def combine_kernel(quarter, ids, routes, weights, rows, hidden, grad, *rest):
    layer_out, gate_grad = rest[-2:]
    tokens, top = ids.shape
    slots = routes.shape[1]
    parts = jnp.dot(weights[...], rows[...], preferred_element_type=F32)
    total = parts[:tokens] + parts[tokens : 2 * tokens] + parts[2 * tokens :]
    layer_out[...] = (hidden[...].astype(F32) + total).astype(BF16)
    dots = lax.dot_general(
        grad[...], rows[...], (((1,), (1,)), ((), ())), preferred_element_type=F32
    )
    dots = jnp.where(routes[...].astype(F32) > 0.0, dots, 0.0)
    expert = lax.broadcasted_iota(jnp.int32, (tokens, slots), 1) // 8
    column = lax.broadcasted_iota(jnp.int32, (tokens, top), 1)
    found = jnp.zeros((tokens, top), F32)
    for k in range(top):
        mine = jnp.sum(jnp.where(expert == ids[:, k : k + 1], dots, 0.0), axis=1, keepdims=True)
        found = found + jnp.where(column == k, mine, 0.0)
    gate_grad[...] = found


def norm_grad_kernel(quarter, routes, rows, hidden, gain, grad, own_grad, gain_part, total):
    step = pl.program_id(0)

    @pl.when(step == 0)
    def _():
        total[...] = jnp.zeros_like(total)

    total[...] += jnp.dot(routes[...], rows[...], preferred_element_type=F32)

    @pl.when(step == pl.num_programs(0) - 1)
    def _():
        values = hidden[...].astype(F32)
        inverse = lax.rsqrt(jnp.mean(values * values, axis=-1, keepdims=True) + epsilon)
        unit = values * inverse
        summed = total[...]
        gain_part[...] = jnp.sum(summed * unit, axis=0, keepdims=True)
        upstream = summed * gain[...]
        own_grad[...] = (
            grad[...].astype(F32)
            + inverse * (upstream - unit * jnp.mean(upstream * unit, axis=-1, keepdims=True))
        ).astype(BF16)


def exchange(block):
    return lax.all_to_all(block, AXES, split_axis=0, concat_axis=0, tiled=True)


def after(value, *earlier):
    return lax.optimization_barrier((value, *earlier))[0]


def params():
    return pltpu.CompilerParams(vmem_limit_bytes=VMEM_LIMIT)


def cost(flops, moved):
    return pl.CostEstimate(flops=flops, bytes_accessed=moved, transcendentals=0)


def dot(a, b, dims):
    return lax.dot_general(a, b, (dims, ((), ())), preferred_element_type=F32)


def per_device(
    hidden, norm_gain, expert_ids, gate_probs, out_grad, gate_weight, up_weight, down_weight
):
    own, width = out_grad.shape
    top = expert_ids.shape[1]
    devices = lax.axis_size(AXES)
    cap = 8
    slots = devices * cap
    steps = 4
    quarter = lax.axis_index("tensor").astype(jnp.int32).reshape(1)
    gain = norm_gain.reshape(1, width)
    ids_t = expert_ids.T
    probs_t = gate_probs.T

    def whole(*shape):
        return pl.BlockSpec(shape, lambda *_: (0,) * len(shape))

    normed_buf = pl.pallas_call(
        pack_normed_kernel,
        grid_spec=pltpu.PrefetchScalarGridSpec(
            num_scalar_prefetch=1,
            grid=(steps,),
            in_specs=[
                whole(top, own),
                pl.BlockSpec((own, width), lambda i, q: (q[0], 0)),
                whole(1, width),
            ],
            out_specs=pl.BlockSpec((slots // steps, width), lambda i, q: (i, 0)),
            scratch_shapes=[pltpu.VMEM((own, width), BF16)],
        ),
        out_shape=jax.ShapeDtypeStruct((slots, width), BF16),
        compiler_params=params(),
        cost_estimate=cost(2 * slots * own * width, 2 * slots * width),
        name="pack_normed",
    )(quarter, ids_t, hidden, gain)
    inputs = exchange(normed_buf)

    scaled_buf = pl.pallas_call(
        pack_scaled_kernel,
        grid=(steps,),
        in_specs=[whole(top, own), whole(top, own), whole(own, width)],
        out_specs=pl.BlockSpec((slots // steps, width), lambda i: (i, 0)),
        out_shape=jax.ShapeDtypeStruct((slots, width), BF16),
        compiler_params=params(),
        cost_estimate=cost(2 * slots * own * width, 2 * slots * width),
        name="pack_scaled",
    )(after(ids_t, normed_buf), probs_t, out_grad)
    cotan = exchange(after(scaled_buf, inputs))

    routes, weights = pl.pallas_call(
        routes_kernel,
        out_shape=[
            jax.ShapeDtypeStruct((own, slots), BF16),
            jax.ShapeDtypeStruct((3 * own, slots), BF16),
        ],
        compiler_params=params(),
        cost_estimate=cost(2 * 4 * own * devices * slots, 8 * own * slots),
        name="routes",
    )(after(expert_ids, normed_buf), gate_probs)

    gate_w, up_w, down_w = gate_weight[0], up_weight[0], down_weight[0]
    gate_pre = dot(inputs, gate_w, ((1,), (0,)))
    up_pre = dot(inputs, up_w, ((1,), (0,)))
    sigma = jax.nn.sigmoid(gate_pre)
    silu_vals = gate_pre * sigma
    act = (silu_vals * up_pre).astype(BF16)
    half = width // 2
    result_a = dot(act, down_w[:, :half], ((1,), (0,))).astype(BF16)
    result_b = dot(act, down_w[:, half:], ((1,), (0,))).astype(BF16)
    returned_a = exchange(after(result_a, cotan))

    act_grad = dot(cotan, down_w, ((1,), (1,)))
    gate_pgrad = (act_grad * up_pre * sigma * (1.0 + gate_pre * (1.0 - sigma))).astype(BF16)
    up_pgrad = (act_grad * silu_vals).astype(BF16)
    back = dot(gate_pgrad, gate_w, ((1,), (1,))) + dot(up_pgrad, up_w, ((1,), (1,)))
    back = back.astype(BF16)
    back_rows = exchange(after(back, returned_a))
    returned_b = exchange(after(result_b, back_rows))

    gate_pgrad, up_pgrad, act_late = lax.optimization_barrier(
        (gate_pgrad, up_pgrad, act, back)
    )[:3]
    gate_wgrad = dot(inputs, gate_pgrad, ((0,), (0,))).astype(BF16)
    up_wgrad = dot(inputs, up_pgrad, ((0,), (0,))).astype(BF16)
    down_grad = dot(act_late, cotan, ((0,), (0,))).astype(BF16)

    def combine(rows, part, earlier):
        columns = rows.shape[1]
        extra = [] if earlier is None else [earlier]
        return pl.pallas_call(
            combine_kernel,
            grid_spec=pltpu.PrefetchScalarGridSpec(
                num_scalar_prefetch=1,
                grid=(1,),
                in_specs=[
                    whole(own, top),
                    whole(own, slots),
                    whole(3 * own, slots),
                    whole(slots, columns),
                    pl.BlockSpec((own, columns), lambda i, q: (q[0], part)),
                    pl.BlockSpec((own, columns), lambda i, q: (0, part)),
                ]
                + [pl.BlockSpec(memory_space=pl.ANY)] * len(extra),
                out_specs=[
                    pl.BlockSpec((own, columns), lambda i, q: (0, part)),
                    whole(own, top),
                ],
            ),
            out_shape=[
                jax.ShapeDtypeStruct((own, width), BF16),
                jax.ShapeDtypeStruct((own, top), F32),
            ],
            input_output_aliases={7: 0} if extra else {},
            compiler_params=params(),
            cost_estimate=cost(8 * own * slots * columns, 2 * slots * columns),
            name=f"combine_{part}",
        )(quarter, expert_ids, routes, weights, rows, hidden, out_grad, *extra)

    layer_out, gate_grad_a = combine(returned_a, 0, None)

    own_grad, gain_part = pl.pallas_call(
        norm_grad_kernel,
        grid_spec=pltpu.PrefetchScalarGridSpec(
            num_scalar_prefetch=1,
            grid=(steps,),
            in_specs=[
                pl.BlockSpec((own, slots // steps), lambda i, q: (0, i)),
                pl.BlockSpec((slots // steps, width), lambda i, q: (i, 0)),
                pl.BlockSpec((own, width), lambda i, q: (q[0], 0)),
                whole(1, width),
                whole(own, width),
            ],
            out_specs=[whole(own, width), whole(1, width)],
            scratch_shapes=[pltpu.VMEM((own, width), F32)],
        ),
        out_shape=[
            jax.ShapeDtypeStruct((own, width), BF16),
            jax.ShapeDtypeStruct((1, width), F32),
        ],
        compiler_params=params(),
        cost_estimate=cost(2 * own * slots * width, 2 * slots * width),
        name="norm_grad",
    )(quarter, routes, back_rows, hidden, gain, out_grad)
    input_grad = lax.all_gather(own_grad, "tensor", axis=0, tiled=True)
    gain_grad = lax.psum(gain_part[0], AXES)

    layer_out, gate_grad_b = combine(returned_b, 1, layer_out)
    gate_grad = gate_grad_a + gate_grad_b
    return (
        layer_out,
        input_grad,
        gate_grad,
        gain_grad,
        gate_wgrad[None],
        up_wgrad[None],
        down_grad[None],
    )


def solution(mesh):
    in_specs = (
        P("dp", None),
        P(),
        P(AXES, None),
        P(AXES, None),
        P(AXES, None),
        P(AXES, None, None),
        P(AXES, None, None),
        P(AXES, None, None),
    )
    out_specs = (
        P(AXES, None),
        P("dp", None),
        P(AXES, None),
        P(),
        P(AXES, None, None),
        P(AXES, None, None),
        P(AXES, None, None),
    )
    return jax.shard_map(
        per_device, mesh=mesh, in_specs=in_specs, out_specs=out_specs, check_vma=False
    )
```

```python
import jax
import jax.numpy as jnp
from jax import lax
from jax.experimental import pallas as pl
from jax.experimental.pallas import tpu as pltpu
from jax.sharding import PartitionSpec as P

epsilon = 1e-06
AXES = ("dp", "tensor")
BF16 = jnp.bfloat16
F32 = jnp.float32
VMEM_LIMIT = 60 * 1024 * 1024


def slot_rows(ids_t, first, count, cap):
    top, tokens = ids_t.shape
    names = lax.broadcasted_iota(jnp.int32, (count, tokens), 0) + first
    named = jnp.zeros((count, tokens), F32)
    for k in range(top):
        named = named + jnp.where(ids_t[k : k + 1, :] == names, 1.0, 0.0)
    before = jnp.where(
        lax.broadcasted_iota(jnp.int32, (tokens, tokens), 0)
        < lax.broadcasted_iota(jnp.int32, (tokens, tokens), 1),
        1.0,
        0.0,
    ).astype(BF16)
    rank = jnp.dot(named.astype(BF16), before, preferred_element_type=F32)
    rank = jnp.where(named > 0.0, rank, -1.0)
    place = lax.broadcasted_iota(jnp.int32, (count, cap, tokens), 1).astype(F32)
    return jnp.where(rank[:, None, :] == place, 1.0, 0.0)


def pack_normed_kernel(quarter, ids_t, hidden, gain, buf, normed):
    step = pl.program_id(0)
    rows, count, cap = buf.shape[0], buf.shape[0] // 8, 8

    @pl.when(step == 0)
    def _():
        values = hidden[...].astype(F32)
        inverse = lax.rsqrt(jnp.mean(values * values, axis=-1, keepdims=True) + epsilon)
        normed[...] = (values * inverse * gain[...]).astype(BF16)

    chosen = slot_rows(ids_t[...], step * count, count, cap).reshape(rows, -1).astype(BF16)
    buf[...] = jnp.dot(chosen, normed[...], preferred_element_type=F32).astype(BF16)


def pack_scaled_kernel(ids_t, probs_t, grad, buf):
    step = pl.program_id(0)
    rows, count, cap = buf.shape[0], buf.shape[0] // 8, 8
    ids = ids_t[...]
    top, tokens = ids.shape
    chosen = slot_rows(ids, step * count, count, cap)
    names = lax.broadcasted_iota(jnp.int32, (count, tokens), 0) + step * count
    prob = jnp.zeros((count, tokens), F32)
    for k in range(top):
        prob = prob + jnp.where(ids[k : k + 1, :] == names, probs_t[k : k + 1, :], 0.0)
    weight = jnp.sum((chosen * prob[:, None, :]).reshape(rows, tokens), axis=1, keepdims=True)
    picked = jnp.dot(
        chosen.reshape(rows, tokens).astype(BF16), grad[...], preferred_element_type=F32
    )
    buf[...] = (picked * weight).astype(BF16)


def routes_kernel(ids, probs, routes, weights):
    tokens, top = ids.shape
    slots = routes.shape[1]
    cap = 8
    experts = slots // cap
    names = lax.broadcasted_iota(jnp.int32, (tokens, experts), 1)
    named = jnp.zeros((tokens, experts), F32)
    prob = jnp.zeros((tokens, experts), F32)
    for k in range(top):
        hit = ids[:, k : k + 1] == names
        named = named + jnp.where(hit, 1.0, 0.0)
        prob = prob + jnp.where(hit, probs[:, k : k + 1], 0.0)
    before = jnp.where(
        lax.broadcasted_iota(jnp.int32, (tokens, tokens), 1)
        < lax.broadcasted_iota(jnp.int32, (tokens, tokens), 0),
        1.0,
        0.0,
    ).astype(BF16)
    rank = jnp.dot(before, named.astype(BF16), preferred_element_type=F32)
    rank = jnp.where(named > 0.0, rank, -1.0).astype(BF16)
    spread = jnp.where(
        lax.broadcasted_iota(jnp.int32, (experts, slots), 1) // cap
        == lax.broadcasted_iota(jnp.int32, (experts, slots), 0),
        1.0,
        0.0,
    ).astype(BF16)
    place = (lax.broadcasted_iota(jnp.int32, (tokens, slots), 1) % cap).astype(F32)
    chosen = jnp.where(
        jnp.dot(rank, spread, preferred_element_type=F32) == place, 1.0, 0.0
    )
    routes[...] = chosen.astype(BF16)
    left = prob
    for part in range(3):
        piece = left.astype(BF16)
        left = left - piece.astype(F32)
        weights[part * tokens : (part + 1) * tokens, :] = (
            chosen * jnp.dot(piece, spread, preferred_element_type=F32)
        ).astype(BF16)


def combine_kernel(
    quarter, ids, routes, weights, rows, hidden, grad, layer_out, gate_grad, dots
):
    step = pl.program_id(0)
    tokens, top = ids.shape
    slots = routes.shape[1]
    parts = jnp.dot(weights[...], rows[...], preferred_element_type=F32)
    total = parts[:tokens] + parts[tokens : 2 * tokens] + parts[2 * tokens :]
    layer_out[...] = (hidden[...].astype(F32) + total).astype(BF16)
    part = lax.dot_general(
        grad[...], rows[...], (((1,), (1,)), ((), ())), preferred_element_type=F32
    )

    @pl.when(step == 0)
    def _():
        dots[...] = part

    @pl.when(step > 0)
    def _():
        dots[...] += part

    @pl.when(step == pl.num_programs(0) - 1)
    def _():
        mine = jnp.where(routes[...].astype(F32) > 0.0, dots[...], 0.0)
        expert = lax.broadcasted_iota(jnp.int32, (tokens, slots), 1) // 8
        column = lax.broadcasted_iota(jnp.int32, (tokens, 128), 1)
        found = jnp.zeros((tokens, 128), F32)
        for k in range(top):
            own = jnp.where(expert == ids[:, k : k + 1], mine, 0.0)
            found = found + jnp.where(column == k, jnp.sum(own, axis=1, keepdims=True), 0.0)
        gate_grad[...] = found.T[:top, :]


def norm_grad_kernel(quarter, routes, rows, hidden, gain, grad, own_grad, gain_part, total):
    step = pl.program_id(0)

    @pl.when(step == 0)
    def _():
        total[...] = jnp.zeros_like(total)

    total[...] += jnp.dot(routes[...], rows[...], preferred_element_type=F32)

    @pl.when(step == pl.num_programs(0) - 1)
    def _():
        values = hidden[...].astype(F32)
        inverse = lax.rsqrt(jnp.mean(values * values, axis=-1, keepdims=True) + epsilon)
        unit = values * inverse
        summed = total[...]
        gain_part[...] = jnp.sum(summed * unit, axis=0, keepdims=True)
        upstream = summed * gain[...]
        own_grad[...] = (
            grad[...].astype(F32)
            + inverse * (upstream - unit * jnp.mean(upstream * unit, axis=-1, keepdims=True))
        ).astype(BF16)


def exchange(block):
    return lax.all_to_all(block, AXES, split_axis=0, concat_axis=0, tiled=True)


def gather_group(block):
    size = lax.axis_size("tensor")
    mine = lax.axis_index("tensor")
    rows = block.shape[0]
    whole = jnp.zeros((size * rows, block.shape[1]), block.dtype)
    moved = [(0, block)] + [
        (step, lax.ppermute(block, "tensor", [(i, (i + step) % size) for i in range(size)]))
        for step in (1, 3, 2)
    ]
    for step, piece in moved:
        origin = (mine - step) % size
        whole = lax.dynamic_update_slice_in_dim(whole, piece, origin * rows, 0)
    return whole


def sum_all(value):
    for axis in AXES:
        size = lax.axis_size(axis)
        step = 1
        while step < size:
            value = value + lax.ppermute(value, axis, [(i, i ^ step) for i in range(size)])
            step *= 2
    return value


def after(value, *earlier):
    return lax.optimization_barrier((value, *earlier))[0]


def params():
    return pltpu.CompilerParams(vmem_limit_bytes=VMEM_LIMIT)


def cost(flops, moved):
    return pl.CostEstimate(flops=flops, bytes_accessed=moved, transcendentals=0)


def dot(a, b, dims):
    return lax.dot_general(a, b, (dims, ((), ())), preferred_element_type=F32)


def per_device(
    hidden, norm_gain, expert_ids, gate_probs, out_grad, gate_weight, up_weight, down_weight
):
    own, width = out_grad.shape
    top = expert_ids.shape[1]
    devices = lax.axis_size(AXES)
    cap = 8
    slots = devices * cap
    steps = 4
    quarter = lax.axis_index("tensor").astype(jnp.int32).reshape(1)
    gain = norm_gain.reshape(1, width)
    ids_t = expert_ids.T
    probs_t = gate_probs.T

    def whole(*shape):
        return pl.BlockSpec(shape, lambda *_: (0,) * len(shape))

    normed_buf = pl.pallas_call(
        pack_normed_kernel,
        grid_spec=pltpu.PrefetchScalarGridSpec(
            num_scalar_prefetch=1,
            grid=(steps,),
            in_specs=[
                whole(top, own),
                pl.BlockSpec((own, width), lambda i, q: (q[0], 0)),
                whole(1, width),
            ],
            out_specs=pl.BlockSpec((slots // steps, width), lambda i, q: (i, 0)),
            scratch_shapes=[pltpu.VMEM((own, width), BF16)],
        ),
        out_shape=jax.ShapeDtypeStruct((slots, width), BF16),
        compiler_params=params(),
        cost_estimate=cost(2 * slots * own * width, 2 * slots * width),
        name="pack_normed",
    )(quarter, ids_t, hidden, gain)
    inputs = exchange(normed_buf)

    scaled_buf = pl.pallas_call(
        pack_scaled_kernel,
        grid=(steps,),
        in_specs=[whole(top, own), whole(top, own), whole(own, width)],
        out_specs=pl.BlockSpec((slots // steps, width), lambda i: (i, 0)),
        out_shape=jax.ShapeDtypeStruct((slots, width), BF16),
        compiler_params=params(),
        cost_estimate=cost(2 * slots * own * width, 2 * slots * width),
        name="pack_scaled",
    )(after(ids_t, normed_buf), probs_t, out_grad)
    cotan = exchange(after(scaled_buf, inputs))

    routes, weights = pl.pallas_call(
        routes_kernel,
        out_shape=[
            jax.ShapeDtypeStruct((own, slots), BF16),
            jax.ShapeDtypeStruct((3 * own, slots), BF16),
        ],
        compiler_params=params(),
        cost_estimate=cost(2 * 4 * own * devices * slots, 8 * own * slots),
        name="routes",
    )(after(expert_ids, normed_buf), gate_probs)

    gate_w, up_w, down_w = gate_weight[0], up_weight[0], down_weight[0]
    gate_pre = dot(inputs, gate_w, ((1,), (0,)))
    up_pre = dot(inputs, up_w, ((1,), (0,)))
    sigma = jax.nn.sigmoid(gate_pre)
    silu_vals = gate_pre * sigma
    act = (silu_vals * up_pre).astype(BF16)
    result = dot(act, down_w, ((1,), (0,))).astype(BF16)
    gate_pre, up_pre, act, cotan, result = lax.optimization_barrier(
        (gate_pre, up_pre, act, cotan, result)
    )
    sigma = jax.nn.sigmoid(gate_pre)
    silu_vals = gate_pre * sigma
    act_grad = dot(cotan, down_w, ((1,), (1,)))
    gate_pgrad = (act_grad * up_pre * sigma * (1.0 + gate_pre * (1.0 - sigma))).astype(BF16)
    up_pgrad = (act_grad * silu_vals).astype(BF16)
    back = dot(gate_pgrad, gate_w, ((1,), (1,))) + dot(up_pgrad, up_w, ((1,), (1,)))
    back = back.astype(BF16)
    back_rows = exchange(back)
    returned = exchange(after(result, back_rows))

    gate_pgrad, up_pgrad, act_late = lax.optimization_barrier(
        (gate_pgrad, up_pgrad, act, back)
    )[:3]
    gate_wgrad = dot(inputs, gate_pgrad, ((0,), (0,))).astype(BF16)
    up_wgrad = dot(inputs, up_pgrad, ((0,), (0,))).astype(BF16)
    down_grad = dot(act_late, cotan, ((0,), (0,))).astype(BF16)

    own_grad, gain_part = pl.pallas_call(
        norm_grad_kernel,
        grid_spec=pltpu.PrefetchScalarGridSpec(
            num_scalar_prefetch=1,
            grid=(steps,),
            in_specs=[
                pl.BlockSpec((own, slots // steps), lambda i, q: (0, i)),
                pl.BlockSpec((slots // steps, width), lambda i, q: (i, 0)),
                pl.BlockSpec((own, width), lambda i, q: (q[0], 0)),
                whole(1, width),
                whole(own, width),
            ],
            out_specs=[whole(own, width), whole(1, width)],
            scratch_shapes=[pltpu.VMEM((own, width), F32)],
        ),
        out_shape=[
            jax.ShapeDtypeStruct((own, width), BF16),
            jax.ShapeDtypeStruct((1, width), F32),
        ],
        compiler_params=params(),
        cost_estimate=cost(2 * own * slots * width, 2 * slots * width),
        name="norm_grad",
    )(quarter, routes, back_rows, hidden, gain, out_grad)
    input_grad = gather_group(own_grad)
    gain_grad = sum_all(gain_part)[0]

    parts = 2
    columns = width // parts
    layer_out, gate_grad_t = pl.pallas_call(
        combine_kernel,
        grid_spec=pltpu.PrefetchScalarGridSpec(
            num_scalar_prefetch=1,
            grid=(parts,),
            in_specs=[
                whole(own, top),
                whole(own, slots),
                whole(3 * own, slots),
                pl.BlockSpec((slots, columns), lambda i, q: (0, i)),
                pl.BlockSpec((own, columns), lambda i, q: (q[0], i)),
                pl.BlockSpec((own, columns), lambda i, q: (0, i)),
            ],
            out_specs=[
                pl.BlockSpec((own, columns), lambda i, q: (0, i)),
                whole(top, own),
            ],
            scratch_shapes=[pltpu.VMEM((own, slots), F32)],
        ),
        out_shape=[
            jax.ShapeDtypeStruct((own, width), BF16),
            jax.ShapeDtypeStruct((top, own), F32),
        ],
        compiler_params=params(),
        cost_estimate=cost(8 * own * slots * width, 2 * slots * width),
        name="combine",
    )(quarter, expert_ids, routes, weights, returned, hidden, out_grad)
    return (
        layer_out,
        input_grad,
        gate_grad_t.T,
        gain_grad,
        gate_wgrad[None],
        up_wgrad[None],
        down_grad[None],
    )


def solution(mesh):
    in_specs = (
        P("dp", None),
        P(),
        P(AXES, None),
        P(AXES, None),
        P(AXES, None),
        P(AXES, None, None),
        P(AXES, None, None),
        P(AXES, None, None),
    )
    out_specs = (
        P(AXES, None),
        P("dp", None),
        P(AXES, None),
        P(),
        P(AXES, None, None),
        P(AXES, None, None),
        P(AXES, None, None),
    )
    return jax.shard_map(
        per_device, mesh=mesh, in_specs=in_specs, out_specs=out_specs, check_vma=False
    )
```

```python
import jax
import jax.numpy as jnp
from jax import lax
from jax.experimental import pallas as pl
from jax.experimental.pallas import tpu as pltpu
from jax.sharding import PartitionSpec as P

epsilon = 1e-06
AXES = ("dp", "tensor")
BF16 = jnp.bfloat16
F32 = jnp.float32
VMEM_LIMIT = 60 * 1024 * 1024


def slot_rows(ids_t, first, count, cap):
    top, tokens = ids_t.shape
    names = lax.broadcasted_iota(jnp.int32, (count, tokens), 0) + first
    named = jnp.zeros((count, tokens), F32)
    for k in range(top):
        named = named + jnp.where(ids_t[k : k + 1, :] == names, 1.0, 0.0)
    before = jnp.where(
        lax.broadcasted_iota(jnp.int32, (tokens, tokens), 0)
        < lax.broadcasted_iota(jnp.int32, (tokens, tokens), 1),
        1.0,
        0.0,
    ).astype(BF16)
    rank = jnp.dot(named.astype(BF16), before, preferred_element_type=F32)
    rank = jnp.where(named > 0.0, rank, -1.0)
    place = lax.broadcasted_iota(jnp.int32, (count, cap, tokens), 1).astype(F32)
    return jnp.where(rank[:, None, :] == place, 1.0, 0.0)


def pack_kernel(quarter, ids_t, probs_t, hidden, gain, grad, buf, normed):
    step = pl.program_id(0)
    rows, cap = buf.shape[0], 8
    count = rows // cap
    width = hidden.shape[1]

    @pl.when(step == 0)
    def _():
        values = hidden[...].astype(F32)
        inverse = lax.rsqrt(jnp.mean(values * values, axis=-1, keepdims=True) + epsilon)
        normed[...] = (values * inverse * gain[...]).astype(BF16)

    ids = ids_t[...]
    top, tokens = ids.shape
    chosen = slot_rows(ids, step * count, count, cap)
    names = lax.broadcasted_iota(jnp.int32, (count, tokens), 0) + step * count
    prob = jnp.zeros((count, tokens), F32)
    for k in range(top):
        prob = prob + jnp.where(ids[k : k + 1, :] == names, probs_t[k : k + 1, :], 0.0)
    weight = jnp.sum((chosen * prob[:, None, :]).reshape(rows, tokens), axis=1, keepdims=True)
    chosen = chosen.reshape(rows, tokens).astype(BF16)
    buf[:, :width] = jnp.dot(chosen, normed[...], preferred_element_type=F32).astype(BF16)
    picked = jnp.dot(chosen, grad[...], preferred_element_type=F32)
    buf[:, width:] = (picked * weight).astype(BF16)


def expert_kernel(
    inputs, cotan, gate_hbm, up_hbm, down_hbm, back, act, gate_pgrad, up_pgrad,
    gate_w, up_w, down_w, sems,
):
    first = pl.program_id(0) == 0
    copies = [
        pltpu.make_async_copy(source, target, sems.at[n])
        for n, (source, target) in enumerate(
            ((gate_hbm, gate_w), (up_hbm, up_w), (down_hbm, down_w))
        )
    ]

    @pl.when(first)
    def _():
        for copy in copies:
            copy.start()
        copies[0].wait()

    gate_pre = jnp.dot(inputs[...], gate_w[...], preferred_element_type=F32)

    @pl.when(first)
    def _():
        copies[1].wait()

    up_pre = jnp.dot(inputs[...], up_w[...], preferred_element_type=F32)
    sigma = jax.nn.sigmoid(gate_pre)
    silu_vals = gate_pre * sigma
    act[...] = (silu_vals * up_pre).astype(BF16)

    @pl.when(first)
    def _():
        copies[2].wait()

    act_grad = lax.dot_general(
        cotan[...], down_w[...], (((1,), (1,)), ((), ())), preferred_element_type=F32
    )
    gate_g = (act_grad * up_pre * sigma * (1.0 + gate_pre * (1.0 - sigma))).astype(BF16)
    up_g = (act_grad * silu_vals).astype(BF16)
    gate_pgrad[...] = gate_g
    up_pgrad[...] = up_g
    total = lax.dot_general(
        gate_g, gate_w[...], (((1,), (1,)), ((), ())), preferred_element_type=F32
    )
    total += lax.dot_general(
        up_g, up_w[...], (((1,), (1,)), ((), ())), preferred_element_type=F32
    )
    back[...] = total.astype(BF16)


def routes_kernel(ids, probs, routes, weights):
    tokens, top = ids.shape
    slots = routes.shape[1]
    cap = 8
    experts = slots // cap
    names = lax.broadcasted_iota(jnp.int32, (tokens, experts), 1)
    named = jnp.zeros((tokens, experts), F32)
    prob = jnp.zeros((tokens, experts), F32)
    for k in range(top):
        hit = ids[:, k : k + 1] == names
        named = named + jnp.where(hit, 1.0, 0.0)
        prob = prob + jnp.where(hit, probs[:, k : k + 1], 0.0)
    before = jnp.where(
        lax.broadcasted_iota(jnp.int32, (tokens, tokens), 1)
        < lax.broadcasted_iota(jnp.int32, (tokens, tokens), 0),
        1.0,
        0.0,
    ).astype(BF16)
    rank = jnp.dot(before, named.astype(BF16), preferred_element_type=F32)
    rank = jnp.where(named > 0.0, rank, -1.0).astype(BF16)
    spread = jnp.where(
        lax.broadcasted_iota(jnp.int32, (experts, slots), 1) // cap
        == lax.broadcasted_iota(jnp.int32, (experts, slots), 0),
        1.0,
        0.0,
    ).astype(BF16)
    place = (lax.broadcasted_iota(jnp.int32, (tokens, slots), 1) % cap).astype(F32)
    chosen = jnp.where(
        jnp.dot(rank, spread, preferred_element_type=F32) == place, 1.0, 0.0
    )
    routes[...] = chosen.astype(BF16)
    left = prob
    for part in range(3):
        piece = left.astype(BF16)
        left = left - piece.astype(F32)
        weights[part * tokens : (part + 1) * tokens, :] = (
            chosen * jnp.dot(piece, spread, preferred_element_type=F32)
        ).astype(BF16)


def combine_kernel(
    quarter, ids, routes, weights, rows, hidden, grad, layer_out, gate_grad, dots
):
    step = pl.program_id(0)
    tokens, top = ids.shape
    slots = routes.shape[1]
    parts = jnp.dot(weights[...], rows[...], preferred_element_type=F32)
    total = parts[:tokens] + parts[tokens : 2 * tokens] + parts[2 * tokens :]
    layer_out[...] = (hidden[...].astype(F32) + total).astype(BF16)
    part = lax.dot_general(
        grad[...], rows[...], (((1,), (1,)), ((), ())), preferred_element_type=F32
    )

    @pl.when(step == 0)
    def _():
        dots[...] = part

    @pl.when(step > 0)
    def _():
        dots[...] += part

    @pl.when(step == pl.num_programs(0) - 1)
    def _():
        mine = jnp.where(routes[...].astype(F32) > 0.0, dots[...], 0.0)
        expert = lax.broadcasted_iota(jnp.int32, (tokens, slots), 1) // 8
        column = lax.broadcasted_iota(jnp.int32, (tokens, 128), 1)
        found = jnp.zeros((tokens, 128), F32)
        for k in range(top):
            own = jnp.where(expert == ids[:, k : k + 1], mine, 0.0)
            found = found + jnp.where(column == k, jnp.sum(own, axis=1, keepdims=True), 0.0)
        gate_grad[...] = found.T[:top, :]


def norm_grad_kernel(quarter, routes, rows, hidden, gain, grad, own_grad, gain_part, total):
    step = pl.program_id(0)

    @pl.when(step == 0)
    def _():
        total[...] = jnp.zeros_like(total)

    total[...] += jnp.dot(routes[...], rows[...], preferred_element_type=F32)

    @pl.when(step == pl.num_programs(0) - 1)
    def _():
        values = hidden[...].astype(F32)
        inverse = lax.rsqrt(jnp.mean(values * values, axis=-1, keepdims=True) + epsilon)
        unit = values * inverse
        summed = total[...]
        gain_part[...] = jnp.sum(summed * unit, axis=0, keepdims=True)
        upstream = summed * gain[...]
        own_grad[...] = (
            grad[...].astype(F32)
            + inverse * (upstream - unit * jnp.mean(upstream * unit, axis=-1, keepdims=True))
        ).astype(BF16)


def exchange(block):
    return lax.all_to_all(block, AXES, split_axis=0, concat_axis=0, tiled=True)


def gather_group(block):
    size = lax.axis_size("tensor")
    mine = lax.axis_index("tensor")
    rows = block.shape[0]
    whole = jnp.zeros((size * rows, block.shape[1]), block.dtype)
    moved = [(0, block)] + [
        (step, lax.ppermute(block, "tensor", [(i, (i + step) % size) for i in range(size)]))
        for step in (1, 3, 2)
    ]
    for step, piece in moved:
        origin = (mine - step) % size
        whole = lax.dynamic_update_slice_in_dim(whole, piece, origin * rows, 0)
    return whole


def sum_all(value):
    def exchange_sum(value, axis, shifts, target):
        size = lax.axis_size(axis)
        others = [
            lax.ppermute(value, axis, [(i, target(i, shift)) for i in range(size)])
            for shift in shifts
        ]
        for other in others:
            value = value + other
        return value

    value = exchange_sum(value, "dp", (1,), lambda i, s: i ^ s)
    value = exchange_sum(value, "tensor", (1, 2, 3), lambda i, s: i ^ s)
    value = exchange_sum(value, "dp", (2, 4, 6), lambda i, s: i ^ s)
    return exchange_sum(value, "dp", (8, 16, 24), lambda i, s: i ^ s)


def after(value, *earlier):
    return lax.optimization_barrier((value, *earlier))[0]


def params():
    return pltpu.CompilerParams(vmem_limit_bytes=VMEM_LIMIT)


def cost(flops, moved):
    return pl.CostEstimate(flops=flops, bytes_accessed=moved, transcendentals=0)


def dot(a, b, dims):
    return lax.dot_general(a, b, (dims, ((), ())), preferred_element_type=F32)


def per_device(
    hidden, norm_gain, expert_ids, gate_probs, out_grad, gate_weight, up_weight, down_weight
):
    own, width = out_grad.shape
    top = expert_ids.shape[1]
    devices = lax.axis_size(AXES)
    cap = 8
    slots = devices * cap
    steps = 4
    quarter = lax.axis_index("tensor").astype(jnp.int32).reshape(1)
    gain = norm_gain.reshape(1, width)
    ids_t = expert_ids.T
    probs_t = gate_probs.T

    def whole(*shape):
        return pl.BlockSpec(shape, lambda *_: (0,) * len(shape))

    pack_steps = 8
    buf = pl.pallas_call(
        pack_kernel,
        grid_spec=pltpu.PrefetchScalarGridSpec(
            num_scalar_prefetch=1,
            grid=(pack_steps,),
            in_specs=[
                whole(top, own),
                whole(top, own),
                pl.BlockSpec((own, width), lambda i, q: (q[0], 0)),
                whole(1, width),
                whole(own, width),
            ],
            out_specs=pl.BlockSpec((slots // pack_steps, 2 * width), lambda i, q: (i, 0)),
            scratch_shapes=[pltpu.VMEM((own, width), BF16)],
        ),
        out_shape=jax.ShapeDtypeStruct((slots, 2 * width), BF16),
        compiler_params=params(),
        cost_estimate=cost(4 * slots * own * width, 4 * slots * width),
        name="pack",
    )(quarter, ids_t, probs_t, hidden, gain, out_grad)
    received = exchange(buf)

    routes, weights = pl.pallas_call(
        routes_kernel,
        out_shape=[
            jax.ShapeDtypeStruct((own, slots), BF16),
            jax.ShapeDtypeStruct((3 * own, slots), BF16),
        ],
        compiler_params=params(),
        cost_estimate=cost(2 * 4 * own * devices * slots, 8 * own * slots),
        name="routes",
    )(after(expert_ids, buf), gate_probs)

    gate_w, up_w, down_w = gate_weight[0], up_weight[0], down_weight[0]
    hidden_units = gate_w.shape[1]
    block = slots // steps

    def row_block(columns, place=0):
        return pl.BlockSpec((block, columns), lambda i: (i, place))

    hbm = pl.BlockSpec(memory_space=pl.ANY)
    back, act, gate_pgrad, up_pgrad = pl.pallas_call(
        expert_kernel,
        grid=(steps,),
        in_specs=[row_block(width), row_block(width, 1), hbm, hbm, hbm],
        out_specs=[
            row_block(width),
            row_block(hidden_units),
            row_block(hidden_units),
            row_block(hidden_units),
        ],
        out_shape=[
            jax.ShapeDtypeStruct((slots, width), BF16),
            jax.ShapeDtypeStruct((slots, hidden_units), BF16),
            jax.ShapeDtypeStruct((slots, hidden_units), BF16),
            jax.ShapeDtypeStruct((slots, hidden_units), BF16),
        ],
        scratch_shapes=[
            pltpu.VMEM(gate_w.shape, BF16),
            pltpu.VMEM(up_w.shape, BF16),
            pltpu.VMEM(down_w.shape, BF16),
            pltpu.SemaphoreType.DMA((3,)),
        ],
        compiler_params=params(),
        cost_estimate=cost(10 * slots * width * hidden_units, 12 * slots * width),
        name="expert",
    )(received, received, gate_w, up_w, down_w)
    back_rows = exchange(back)

    result = dot(act, down_w, ((1,), (0,))).astype(BF16)
    inputs, cotan = received[:, :width], received[:, width:]
    gate_wgrad = dot(inputs, gate_pgrad, ((0,), (0,))).astype(BF16)
    up_wgrad = dot(inputs, up_pgrad, ((0,), (0,))).astype(BF16)
    down_grad = dot(act, cotan, ((0,), (0,))).astype(BF16)
    result, gate_wgrad, up_wgrad, down_grad, back_rows, routes, weights = (
        lax.optimization_barrier(
            (result, gate_wgrad, up_wgrad, down_grad, back_rows, routes, weights)
        )
    )
    returned = exchange(result)

    own_grad, gain_part = pl.pallas_call(
        norm_grad_kernel,
        grid_spec=pltpu.PrefetchScalarGridSpec(
            num_scalar_prefetch=1,
            grid=(steps,),
            in_specs=[
                pl.BlockSpec((own, slots // steps), lambda i, q: (0, i)),
                pl.BlockSpec((slots // steps, width), lambda i, q: (i, 0)),
                pl.BlockSpec((own, width), lambda i, q: (q[0], 0)),
                whole(1, width),
                whole(own, width),
            ],
            out_specs=[whole(own, width), whole(1, width)],
            scratch_shapes=[pltpu.VMEM((own, width), F32)],
        ),
        out_shape=[
            jax.ShapeDtypeStruct((own, width), BF16),
            jax.ShapeDtypeStruct((1, width), F32),
        ],
        compiler_params=params(),
        cost_estimate=cost(2 * own * slots * width, 2 * slots * width),
        name="norm_grad",
    )(quarter, routes, back_rows, hidden, gain, out_grad)
    input_grad = gather_group(own_grad)
    gain_grad = sum_all(gain_part)[0]

    parts = 4
    columns = width // parts
    layer_out, gate_grad_t = pl.pallas_call(
        combine_kernel,
        grid_spec=pltpu.PrefetchScalarGridSpec(
            num_scalar_prefetch=1,
            grid=(parts,),
            in_specs=[
                whole(own, top),
                whole(own, slots),
                whole(3 * own, slots),
                pl.BlockSpec((slots, columns), lambda i, q: (0, i)),
                pl.BlockSpec((own, columns), lambda i, q: (q[0], i)),
                pl.BlockSpec((own, columns), lambda i, q: (0, i)),
            ],
            out_specs=[
                pl.BlockSpec((own, columns), lambda i, q: (0, i)),
                whole(top, own),
            ],
            scratch_shapes=[pltpu.VMEM((own, slots), F32)],
        ),
        out_shape=[
            jax.ShapeDtypeStruct((own, width), BF16),
            jax.ShapeDtypeStruct((top, own), F32),
        ],
        compiler_params=params(),
        cost_estimate=cost(8 * own * slots * width, 2 * slots * width),
        name="combine",
    )(quarter, expert_ids, routes, weights, returned, hidden, out_grad)
    return (
        layer_out,
        input_grad,
        gate_grad_t.T,
        gain_grad,
        gate_wgrad[None],
        up_wgrad[None],
        down_grad[None],
    )


def solution(mesh):
    in_specs = (
        P("dp", None),
        P(),
        P(AXES, None),
        P(AXES, None),
        P(AXES, None),
        P(AXES, None, None),
        P(AXES, None, None),
        P(AXES, None, None),
    )
    out_specs = (
        P(AXES, None),
        P("dp", None),
        P(AXES, None),
        P(),
        P(AXES, None, None),
        P(AXES, None, None),
        P(AXES, None, None),
    )
    return jax.shard_map(
        per_device, mesh=mesh, in_specs=in_specs, out_specs=out_specs, check_vma=False
    )
```

```python
import jax
import jax.numpy as jnp
from jax import lax
from jax.experimental import pallas as pl
from jax.experimental.pallas import tpu as pltpu
from jax.sharding import PartitionSpec as P

epsilon = 1e-06
AXES = ("dp", "tensor")
BF16 = jnp.bfloat16
F32 = jnp.float32
VMEM_LIMIT = 60 * 1024 * 1024


def slot_rows(ids_t, first, count, cap):
    top, tokens = ids_t.shape
    names = lax.broadcasted_iota(jnp.int32, (count, tokens), 0) + first
    named = jnp.zeros((count, tokens), F32)
    for k in range(top):
        named = named + jnp.where(ids_t[k : k + 1, :] == names, 1.0, 0.0)
    before = jnp.where(
        lax.broadcasted_iota(jnp.int32, (tokens, tokens), 0)
        < lax.broadcasted_iota(jnp.int32, (tokens, tokens), 1),
        1.0,
        0.0,
    ).astype(BF16)
    rank = jnp.dot(named.astype(BF16), before, preferred_element_type=F32)
    rank = jnp.where(named > 0.0, rank, -1.0)
    place = lax.broadcasted_iota(jnp.int32, (count, cap, tokens), 1).astype(F32)
    return jnp.where(rank[:, None, :] == place, 1.0, 0.0)


def pack_kernel(quarter, ids_t, probs_t, hidden, gain, grad, out, buf, sems):
    chunks = sems.shape[0]
    rows, cap = out.shape[0] // chunks, 8
    count = rows // cap
    width = hidden.shape[1]
    values = hidden[...].astype(F32)
    inverse = lax.rsqrt(jnp.mean(values * values, axis=-1, keepdims=True) + epsilon)
    normed = (values * inverse * gain[...]).astype(BF16)
    ids = ids_t[...]
    top, tokens = ids.shape
    copies = []
    for chunk in range(chunks):
        chosen = slot_rows(ids, chunk * count, count, cap)
        names = lax.broadcasted_iota(jnp.int32, (count, tokens), 0) + chunk * count
        prob = jnp.zeros((count, tokens), F32)
        for k in range(top):
            prob = prob + jnp.where(ids[k : k + 1, :] == names, probs_t[k : k + 1, :], 0.0)
        weight = jnp.sum(
            (chosen * prob[:, None, :]).reshape(rows, tokens), axis=1, keepdims=True
        )
        chosen = chosen.reshape(rows, tokens).astype(BF16)
        part = pl.ds(chunk * rows, rows)
        buf[part, :width] = jnp.dot(chosen, normed, preferred_element_type=F32).astype(BF16)
        picked = jnp.dot(chosen, grad[...], preferred_element_type=F32)
        buf[part, width:] = (picked * weight).astype(BF16)
        copy = pltpu.make_async_copy(buf.at[part], out.at[part], sems.at[chunk])
        copy.start()
        copies.append(copy)
    for copy in copies:
        copy.wait()


def expert_kernel(
    received, gate_hbm, up_hbm, down_hbm, back, act, gate_pgrad, up_pgrad,
    inputs, cotan, both_w, down_w, back_buf, act_buf, grads_buf, in_sems, out_sems,
):
    blocks = out_sems.shape[0] // 4
    rows = received.shape[0] // blocks
    width = back.shape[1]
    units = act.shape[1]
    weight_copies = [
        pltpu.make_async_copy(gate_hbm, both_w.at[:, pl.ds(0, units)], in_sems.at[0]),
        pltpu.make_async_copy(up_hbm, both_w.at[:, pl.ds(units, units)], in_sems.at[1]),
        pltpu.make_async_copy(down_hbm, down_w, in_sems.at[2]),
    ]
    row_copies = []
    for block in range(blocks):
        part = pl.ds(block * rows, rows)
        for n, target in enumerate((inputs, cotan)):
            row_copies.append(
                pltpu.make_async_copy(
                    received.at[part, pl.ds(n * width, width)],
                    target.at[part],
                    in_sems.at[3 + 2 * block + n],
                )
            )
    for copy in [weight_copies[0], row_copies[0], *weight_copies[1:], *row_copies[1:]]:
        copy.start()
    out_copies = []
    for block in range(blocks):
        part = pl.ds(block * rows, rows)
        row_copies[2 * block].wait()
        if block == 0:
            weight_copies[0].wait()
            weight_copies[1].wait()
        pre = jnp.dot(inputs[part, :], both_w[...], preferred_element_type=F32)
        gate_pre, up_pre = pre[:, :units], pre[:, units:]
        sigma = jax.nn.sigmoid(gate_pre)
        silu_vals = gate_pre * sigma
        act_buf[part, :] = (silu_vals * up_pre).astype(BF16)
        row_copies[2 * block + 1].wait()
        if block == 0:
            weight_copies[2].wait()
        act_grad = lax.dot_general(
            cotan[part, :], down_w[...], (((1,), (1,)), ((), ())), preferred_element_type=F32
        )
        grads_buf[part, :units] = (
            act_grad * up_pre * sigma * (1.0 + gate_pre * (1.0 - sigma))
        ).astype(BF16)
        grads_buf[part, units:] = (act_grad * silu_vals).astype(BF16)
        back_buf[part, :] = lax.dot_general(
            grads_buf[part, :], both_w[...], (((1,), (1,)), ((), ())), preferred_element_type=F32
        ).astype(BF16)
        for n, (source, target) in enumerate(
            (
                (back_buf.at[part], back),
                (act_buf.at[part], act),
                (grads_buf.at[part, pl.ds(0, units)], gate_pgrad),
                (grads_buf.at[part, pl.ds(units, units)], up_pgrad),
            )
        ):
            copy = pltpu.make_async_copy(source, target.at[part], out_sems.at[4 * block + n])
            copy.start()
            out_copies.append(copy)
    for copy in out_copies:
        copy.wait()


def routes_kernel(ids, probs, routes, weights):
    tokens, top = ids.shape
    slots = routes.shape[1]
    cap = 8
    experts = slots // cap
    names = lax.broadcasted_iota(jnp.int32, (tokens, experts), 1)
    named = jnp.zeros((tokens, experts), F32)
    prob = jnp.zeros((tokens, experts), F32)
    for k in range(top):
        hit = ids[:, k : k + 1] == names
        named = named + jnp.where(hit, 1.0, 0.0)
        prob = prob + jnp.where(hit, probs[:, k : k + 1], 0.0)
    before = jnp.where(
        lax.broadcasted_iota(jnp.int32, (tokens, tokens), 1)
        < lax.broadcasted_iota(jnp.int32, (tokens, tokens), 0),
        1.0,
        0.0,
    ).astype(BF16)
    rank = jnp.dot(before, named.astype(BF16), preferred_element_type=F32)
    rank = jnp.where(named > 0.0, rank, -1.0).astype(BF16)
    spread = jnp.where(
        lax.broadcasted_iota(jnp.int32, (experts, slots), 1) // cap
        == lax.broadcasted_iota(jnp.int32, (experts, slots), 0),
        1.0,
        0.0,
    ).astype(BF16)
    place = (lax.broadcasted_iota(jnp.int32, (tokens, slots), 1) % cap).astype(F32)
    chosen = jnp.where(
        jnp.dot(rank, spread, preferred_element_type=F32) == place, 1.0, 0.0
    )
    routes[...] = chosen.astype(BF16)
    left = prob
    for part in range(3):
        piece = left.astype(BF16)
        left = left - piece.astype(F32)
        weights[part * tokens : (part + 1) * tokens, :] = (
            chosen * jnp.dot(piece, spread, preferred_element_type=F32)
        ).astype(BF16)


def combine_kernel(
    quarter, ids, routes, weights, rows, hidden, grad, layer_out, gate_grad, total, found
):
    step = pl.program_id(0)
    tokens, top = ids.shape
    slots = rows.shape[0]

    @pl.when(step == 0)
    def _():
        total[...] = hidden[...].astype(F32)
        found[...] = jnp.zeros_like(found)

    parts = jnp.dot(weights[...], rows[...], preferred_element_type=F32)
    total[...] += parts[:tokens] + parts[tokens : 2 * tokens] + parts[2 * tokens :]
    dots = lax.dot_general(
        rows[...], grad[...], (((1,), (1,)), ((), ())), preferred_element_type=F32
    ).T
    mine = jnp.where(routes[...].astype(F32) > 0.0, dots, 0.0)
    expert = (lax.broadcasted_iota(jnp.int32, (tokens, slots), 1) + step * slots) // 8
    column = lax.broadcasted_iota(jnp.int32, found.shape, 1)
    sums = found[...]
    for k in range(top):
        own = jnp.where(expert == ids[:, k : k + 1], mine, 0.0)
        sums = sums + jnp.where(column == k, jnp.sum(own, axis=1, keepdims=True), 0.0)
    found[...] = sums

    @pl.when(step == pl.num_programs(0) - 1)
    def _():
        layer_out[...] = total[...].astype(BF16)
        gate_grad[...] = found[...].T[:top, :]


def norm_grad_kernel(quarter, routes, rows, hidden, gain, grad, own_grad, total):
    step = pl.program_id(0)

    @pl.when(step == 0)
    def _():
        total[...] = jnp.zeros_like(total)

    total[...] += jnp.dot(routes[...], rows[...], preferred_element_type=F32)

    @pl.when(step == pl.num_programs(0) - 1)
    def _():
        values = hidden[...].astype(F32)
        inverse = lax.rsqrt(jnp.mean(values * values, axis=-1, keepdims=True) + epsilon)
        unit = values * inverse
        summed = total[...]
        upstream = summed * gain[...]
        own_grad[...] = (
            grad[...].astype(F32)
            + inverse * (upstream - unit * jnp.mean(upstream * unit, axis=-1, keepdims=True))
        ).astype(BF16)


def exchange(block):
    return lax.all_to_all(block, AXES, split_axis=0, concat_axis=0, tiled=True)


def gather_group(block):
    size = lax.axis_size("tensor")
    mine = lax.axis_index("tensor")
    rows = block.shape[0]
    whole = jnp.zeros((size * rows, block.shape[1]), block.dtype)
    moved = [(0, block)] + [
        (step, lax.ppermute(block, "tensor", [(i, (i + step) % size) for i in range(size)]))
        for step in (1, 3, 2)
    ]
    for step, piece in moved:
        origin = (mine - step) % size
        whole = lax.dynamic_update_slice_in_dim(whole, piece, origin * rows, 0)
    return whole


def add_from(value, axis, distances):
    size = lax.axis_size(axis)
    others = [
        lax.ppermute(value, axis, [(i, i ^ distance) for i in range(size)])
        for distance in distances
    ]
    for other in others:
        value = value + other
    return value


def after(value, *earlier):
    return lax.optimization_barrier((value, *earlier))[0]


def params():
    return pltpu.CompilerParams(vmem_limit_bytes=VMEM_LIMIT)


def cost(flops, moved):
    return pl.CostEstimate(flops=flops, bytes_accessed=moved, transcendentals=0)


def dot(a, b, dims):
    return lax.dot_general(a, b, (dims, ((), ())), preferred_element_type=F32)


def per_device(
    hidden, norm_gain, expert_ids, gate_probs, out_grad, gate_weight, up_weight, down_weight
):
    own, width = out_grad.shape
    top = expert_ids.shape[1]
    devices = lax.axis_size(AXES)
    cap = 8
    slots = devices * cap
    steps = 4
    quarter = lax.axis_index("tensor").astype(jnp.int32).reshape(1)
    gain = norm_gain.reshape(1, width)
    ids_t = expert_ids.T
    probs_t = gate_probs.T

    def whole(*shape):
        return pl.BlockSpec(shape, lambda *_: (0,) * len(shape))

    hbm = pl.BlockSpec(memory_space=pl.ANY)
    buf = pl.pallas_call(
        pack_kernel,
        grid_spec=pltpu.PrefetchScalarGridSpec(
            num_scalar_prefetch=1,
            grid=(1,),
            in_specs=[
                whole(top, own),
                whole(top, own),
                pl.BlockSpec((own, width), lambda i, q: (q[0], 0)),
                whole(1, width),
                whole(own, width),
            ],
            out_specs=hbm,
            scratch_shapes=[
                pltpu.VMEM((slots, 2 * width), BF16),
                pltpu.SemaphoreType.DMA((steps,)),
            ],
        ),
        out_shape=jax.ShapeDtypeStruct((slots, 2 * width), BF16),
        compiler_params=params(),
        cost_estimate=cost(4 * slots * own * width, 4 * slots * width),
        name="pack",
    )(quarter, ids_t, probs_t, hidden, gain, out_grad)
    received = exchange(buf)

    routes, weights = pl.pallas_call(
        routes_kernel,
        out_shape=[
            jax.ShapeDtypeStruct((own, slots), BF16),
            jax.ShapeDtypeStruct((3 * own, slots), BF16),
        ],
        compiler_params=params(),
        cost_estimate=cost(2 * 4 * own * devices * slots, 8 * own * slots),
        name="routes",
    )(after(expert_ids, buf), gate_probs)

    gate_w, up_w, down_w = gate_weight[0], up_weight[0], down_weight[0]
    units = gate_w.shape[1]
    blocks = 2
    back, act, gate_pgrad, up_pgrad = pl.pallas_call(
        expert_kernel,
        in_specs=[hbm] * 4,
        out_specs=[hbm] * 4,
        out_shape=[
            jax.ShapeDtypeStruct((slots, width), BF16),
            jax.ShapeDtypeStruct((slots, units), BF16),
            jax.ShapeDtypeStruct((slots, units), BF16),
            jax.ShapeDtypeStruct((slots, units), BF16),
        ],
        scratch_shapes=[
            pltpu.VMEM((slots, width), BF16),
            pltpu.VMEM((slots, width), BF16),
            pltpu.VMEM((width, 2 * units), BF16),
            pltpu.VMEM((units, width), BF16),
            pltpu.VMEM((slots, width), BF16),
            pltpu.VMEM((slots, units), BF16),
            pltpu.VMEM((slots, 2 * units), BF16),
            pltpu.SemaphoreType.DMA((3 + 2 * blocks,)),
            pltpu.SemaphoreType.DMA((4 * blocks,)),
        ],
        compiler_params=params(),
        cost_estimate=cost(10 * slots * width * units, 12 * slots * width),
        name="expert",
    )(received, gate_w, up_w, down_w)
    back_rows = exchange(back)

    result = dot(act, down_w, ((1,), (0,))).astype(BF16)
    inputs, cotan = received[:, :width], received[:, width:]
    gate_wgrad = dot(inputs, gate_pgrad, ((0,), (0,))).astype(BF16)
    up_wgrad = dot(inputs, up_pgrad, ((0,), (0,))).astype(BF16)
    down_grad = dot(act, cotan, ((0,), (0,))).astype(BF16)
    gain_part = jnp.sum(back.astype(F32) * inputs.astype(F32), axis=0, keepdims=True) / gain
    gain_part = add_from(gain_part, "dp", (1,))
    gain_part = add_from(gain_part, "tensor", (1, 2, 3))
    gain_part = add_from(gain_part, "dp", (2, 4, 6))
    result, gate_wgrad, up_wgrad, down_grad, back_rows, routes, weights, gain_part = (
        lax.optimization_barrier(
            (result, gate_wgrad, up_wgrad, down_grad, back_rows, routes, weights, gain_part)
        )
    )
    returned = exchange(result)
    gain_grad = add_from(add_from(gain_part, "dp", (8,)), "dp", (16,))[0]

    own_grad = pl.pallas_call(
        norm_grad_kernel,
        grid_spec=pltpu.PrefetchScalarGridSpec(
            num_scalar_prefetch=1,
            grid=(steps,),
            in_specs=[
                pl.BlockSpec((own, slots // steps), lambda i, q: (0, i)),
                pl.BlockSpec((slots // steps, width), lambda i, q: (i, 0)),
                pl.BlockSpec((own, width), lambda i, q: (q[0], 0)),
                whole(1, width),
                whole(own, width),
            ],
            out_specs=whole(own, width),
            scratch_shapes=[pltpu.VMEM((own, width), F32)],
        ),
        out_shape=jax.ShapeDtypeStruct((own, width), BF16),
        compiler_params=params(),
        cost_estimate=cost(2 * own * slots * width, 2 * slots * width),
        name="norm_grad",
    )(quarter, routes, back_rows, hidden, gain, out_grad)
    input_grad = gather_group(own_grad)

    halves = 2
    layer_out, gate_grad_t = pl.pallas_call(
        combine_kernel,
        grid_spec=pltpu.PrefetchScalarGridSpec(
            num_scalar_prefetch=1,
            grid=(halves,),
            in_specs=[
                whole(own, top),
                pl.BlockSpec((own, slots // halves), lambda i, q: (0, i)),
                pl.BlockSpec((3 * own, slots // halves), lambda i, q: (0, i)),
                pl.BlockSpec((slots // halves, width), lambda i, q: (i, 0)),
                pl.BlockSpec((own, width), lambda i, q: (q[0], 0)),
                whole(own, width),
            ],
            out_specs=[whole(own, width), whole(top, own)],
            scratch_shapes=[pltpu.VMEM((own, width), F32), pltpu.VMEM((own, 128), F32)],
        ),
        out_shape=[
            jax.ShapeDtypeStruct((own, width), BF16),
            jax.ShapeDtypeStruct((top, own), F32),
        ],
        compiler_params=params(),
        cost_estimate=cost(8 * own * slots * width, 2 * slots * width),
        name="combine",
    )(quarter, expert_ids, routes, weights, returned, hidden, out_grad)
    return (
        layer_out,
        input_grad,
        gate_grad_t.T,
        gain_grad,
        gate_wgrad[None],
        up_wgrad[None],
        down_grad[None],
    )


def solution(mesh):
    in_specs = (
        P("dp", None),
        P(),
        P(AXES, None),
        P(AXES, None),
        P(AXES, None),
        P(AXES, None, None),
        P(AXES, None, None),
        P(AXES, None, None),
    )
    out_specs = (
        P(AXES, None),
        P("dp", None),
        P(AXES, None),
        P(),
        P(AXES, None, None),
        P(AXES, None, None),
        P(AXES, None, None),
    )
    return jax.shard_map(
        per_device, mesh=mesh, in_specs=in_specs, out_specs=out_specs, check_vma=False
    )
```

```python
import jax
import jax.numpy as jnp
from jax import lax
from jax.experimental import pallas as pl
from jax.experimental.pallas import tpu as pltpu
from jax.sharding import PartitionSpec as P

epsilon = 1e-06
AXES = ("dp", "tensor")
BF16 = jnp.bfloat16
F32 = jnp.float32
VMEM_LIMIT = 60 * 1024 * 1024


def slot_rows(ids_t, first, count, cap):
    top, tokens = ids_t.shape
    names = lax.broadcasted_iota(jnp.int32, (count, tokens), 0) + first
    named = jnp.zeros((count, tokens), F32)
    for k in range(top):
        named = named + jnp.where(ids_t[k : k + 1, :] == names, 1.0, 0.0)
    before = jnp.where(
        lax.broadcasted_iota(jnp.int32, (tokens, tokens), 0)
        < lax.broadcasted_iota(jnp.int32, (tokens, tokens), 1),
        1.0,
        0.0,
    ).astype(BF16)
    rank = jnp.dot(named.astype(BF16), before, preferred_element_type=F32)
    rank = jnp.where(named > 0.0, rank, -1.0)
    place = lax.broadcasted_iota(jnp.int32, (count, cap, tokens), 1).astype(F32)
    return jnp.where(rank[:, None, :] == place, 1.0, 0.0)


def pack_normed_kernel(quarter, ids_t, hidden, gain, out, buf, sems):
    chunks = sems.shape[0]
    rows, cap = out.shape[0] // chunks, 8
    count = rows // cap
    values = hidden[...].astype(F32)
    inverse = lax.rsqrt(jnp.mean(values * values, axis=-1, keepdims=True) + epsilon)
    normed = (values * inverse * gain[...]).astype(BF16)
    ids = ids_t[...]
    copies = []
    for chunk in range(chunks):
        chosen = slot_rows(ids, chunk * count, count, cap).reshape(rows, -1).astype(BF16)
        part = pl.ds(chunk * rows, rows)
        buf[part, :] = jnp.dot(chosen, normed, preferred_element_type=F32).astype(BF16)
        copy = pltpu.make_async_copy(buf.at[part], out.at[part], sems.at[chunk])
        copy.start()
        copies.append(copy)
    for copy in copies:
        copy.wait()


def pack_scaled_kernel(ids_t, probs_t, grad, buf):
    step = pl.program_id(0)
    rows, count, cap = buf.shape[0], buf.shape[0] // 8, 8
    ids = ids_t[...]
    top, tokens = ids.shape
    chosen = slot_rows(ids, step * count, count, cap)
    names = lax.broadcasted_iota(jnp.int32, (count, tokens), 0) + step * count
    prob = jnp.zeros((count, tokens), F32)
    for k in range(top):
        prob = prob + jnp.where(ids[k : k + 1, :] == names, probs_t[k : k + 1, :], 0.0)
    weight = jnp.sum((chosen * prob[:, None, :]).reshape(rows, tokens), axis=1, keepdims=True)
    picked = jnp.dot(
        chosen.reshape(rows, tokens).astype(BF16), grad[...], preferred_element_type=F32
    )
    buf[...] = (picked * weight).astype(BF16)


def routes_kernel(ids, probs, routes, weights):
    tokens, top = ids.shape
    slots = routes.shape[1]
    cap = 8
    experts = slots // cap
    names = lax.broadcasted_iota(jnp.int32, (tokens, experts), 1)
    named = jnp.zeros((tokens, experts), F32)
    prob = jnp.zeros((tokens, experts), F32)
    for k in range(top):
        hit = ids[:, k : k + 1] == names
        named = named + jnp.where(hit, 1.0, 0.0)
        prob = prob + jnp.where(hit, probs[:, k : k + 1], 0.0)
    before = jnp.where(
        lax.broadcasted_iota(jnp.int32, (tokens, tokens), 1)
        < lax.broadcasted_iota(jnp.int32, (tokens, tokens), 0),
        1.0,
        0.0,
    ).astype(BF16)
    rank = jnp.dot(before, named.astype(BF16), preferred_element_type=F32)
    rank = jnp.where(named > 0.0, rank, -1.0).astype(BF16)
    spread = jnp.where(
        lax.broadcasted_iota(jnp.int32, (experts, slots), 1) // cap
        == lax.broadcasted_iota(jnp.int32, (experts, slots), 0),
        1.0,
        0.0,
    ).astype(BF16)
    place = (lax.broadcasted_iota(jnp.int32, (tokens, slots), 1) % cap).astype(F32)
    chosen = jnp.where(
        jnp.dot(rank, spread, preferred_element_type=F32) == place, 1.0, 0.0
    )
    routes[...] = chosen.astype(BF16)
    left = prob
    for part in range(3):
        piece = left.astype(BF16)
        left = left - piece.astype(F32)
        weights[part * tokens : (part + 1) * tokens, :] = (
            chosen * jnp.dot(piece, spread, preferred_element_type=F32)
        ).astype(BF16)


def combine_kernel(
    quarter, ids, routes, weights, rows, hidden, grad, layer_out, gate_grad, total, found
):
    step = pl.program_id(0)
    tokens, top = ids.shape
    slots = rows.shape[0]

    @pl.when(step == 0)
    def _():
        total[...] = hidden[...].astype(F32)
        found[...] = jnp.zeros_like(found)

    parts = jnp.dot(weights[...], rows[...], preferred_element_type=F32)
    total[...] += parts[:tokens] + parts[tokens : 2 * tokens] + parts[2 * tokens :]
    dots = lax.dot_general(
        rows[...], grad[...], (((1,), (1,)), ((), ())), preferred_element_type=F32
    ).T
    mine = jnp.where(routes[...].astype(F32) > 0.0, dots, 0.0)
    expert = (lax.broadcasted_iota(jnp.int32, (tokens, slots), 1) + step * slots) // 8
    column = lax.broadcasted_iota(jnp.int32, found.shape, 1)
    sums = found[...]
    for k in range(top):
        own = jnp.where(expert == ids[:, k : k + 1], mine, 0.0)
        sums = sums + jnp.where(column == k, jnp.sum(own, axis=1, keepdims=True), 0.0)
    found[...] = sums

    @pl.when(step == pl.num_programs(0) - 1)
    def _():
        layer_out[...] = total[...].astype(BF16)
        gate_grad[...] = found[...].T[:top, :]


def norm_grad_kernel(quarter, routes, rows, hidden, gain, grad, own_grad, group_grad, total):
    step = pl.program_id(0)
    part = jnp.dot(routes[...], rows[...], preferred_element_type=F32)

    @pl.when(step == 0)
    def _():
        total[...] = part

    @pl.when(step > 0)
    def _():
        total[...] += part

    @pl.when(step == pl.num_programs(0) - 1)
    def _():
        values = hidden[...].astype(F32)
        inverse = lax.rsqrt(jnp.mean(values * values, axis=-1, keepdims=True) + epsilon)
        unit = values * inverse
        upstream = total[...] * gain[...]
        result = (
            grad[...].astype(F32)
            + inverse * (upstream - unit * jnp.mean(upstream * unit, axis=-1, keepdims=True))
        ).astype(BF16)
        own_grad[...] = result
        group_grad[...] = result


def exchange(block):
    return lax.all_to_all(block, AXES, split_axis=0, concat_axis=0, tiled=True)


def gather_group(block, whole):
    size = lax.axis_size("tensor")
    mine = lax.axis_index("tensor")
    rows = block.shape[0]
    moved = [
        (step, lax.ppermute(block, "tensor", [(i, (i + step) % size) for i in range(size)]))
        for step in (1, 3, 2)
    ]
    for step, piece in moved:
        origin = (mine + size - step) % size
        whole = lax.dynamic_update_slice_in_dim(whole, piece, origin * rows, 0)
    return whole


def add_from(value, axis, distances):
    size = lax.axis_size(axis)
    others = [
        lax.ppermute(value, axis, [(i, i ^ distance) for i in range(size)])
        for distance in distances
    ]
    for other in others:
        value = value + other
    return value


def after(value, *earlier):
    return lax.optimization_barrier((value, *earlier))[0]


def params():
    return pltpu.CompilerParams(vmem_limit_bytes=VMEM_LIMIT)


def cost(flops, moved):
    return pl.CostEstimate(flops=flops, bytes_accessed=moved, transcendentals=0)


def dot(a, b, dims):
    return lax.dot_general(a, b, (dims, ((), ())), preferred_element_type=F32)


def per_device(
    hidden, norm_gain, expert_ids, gate_probs, out_grad, gate_weight, up_weight, down_weight
):
    own, width = out_grad.shape
    top = expert_ids.shape[1]
    devices = lax.axis_size(AXES)
    cap = 8
    slots = devices * cap
    steps = 4
    quarter = lax.axis_index("tensor").astype(jnp.int32).reshape(1)
    gain = norm_gain.reshape(1, width)
    ids_t = expert_ids.T
    probs_t = gate_probs.T

    def whole(*shape):
        return pl.BlockSpec(shape, lambda *_: (0,) * len(shape))

    normed_buf = pl.pallas_call(
        pack_normed_kernel,
        grid_spec=pltpu.PrefetchScalarGridSpec(
            num_scalar_prefetch=1,
            grid=(1,),
            in_specs=[
                whole(top, own),
                pl.BlockSpec((own, width), lambda i, q: (q[0], 0)),
                whole(1, width),
            ],
            out_specs=pl.BlockSpec(memory_space=pl.ANY),
            scratch_shapes=[
                pltpu.VMEM((slots, width), BF16),
                pltpu.SemaphoreType.DMA((steps,)),
            ],
        ),
        out_shape=jax.ShapeDtypeStruct((slots, width), BF16),
        compiler_params=params(),
        cost_estimate=cost(2 * slots * own * width, 2 * slots * width),
        name="pack_normed",
    )(quarter, ids_t, hidden, gain)
    inputs = exchange(normed_buf)

    scaled_buf = pl.pallas_call(
        pack_scaled_kernel,
        grid=(steps,),
        in_specs=[whole(top, own), whole(top, own), whole(own, width)],
        out_specs=pl.BlockSpec((slots // steps, width), lambda i: (i, 0)),
        out_shape=jax.ShapeDtypeStruct((slots, width), BF16),
        compiler_params=params(),
        cost_estimate=cost(2 * slots * own * width, 2 * slots * width),
        name="pack_scaled",
    )(after(ids_t, normed_buf), probs_t, out_grad)
    cotan = exchange(after(scaled_buf, inputs))

    routes, weights = pl.pallas_call(
        routes_kernel,
        out_shape=[
            jax.ShapeDtypeStruct((own, slots), BF16),
            jax.ShapeDtypeStruct((3 * own, slots), BF16),
        ],
        compiler_params=params(),
        cost_estimate=cost(2 * 4 * own * devices * slots, 8 * own * slots),
        name="routes",
    )(after(expert_ids, normed_buf), gate_probs)

    gate_w, up_w, down_w = gate_weight[0], up_weight[0], down_weight[0]
    gate_pre = dot(inputs, gate_w, ((1,), (0,)))
    up_pre = dot(inputs, up_w, ((1,), (0,)))
    sigma = jax.nn.sigmoid(gate_pre)
    silu_vals = gate_pre * sigma
    act = (silu_vals * up_pre).astype(BF16)
    result = dot(act, down_w, ((1,), (0,))).astype(BF16)
    gate_pre, up_pre, act, cotan, result = lax.optimization_barrier(
        (gate_pre, up_pre, act, cotan, result)
    )
    returned = exchange(result)

    sigma = jax.nn.sigmoid(gate_pre)
    silu_vals = gate_pre * sigma
    act_grad = dot(cotan, down_w, ((1,), (1,)))
    gate_pgrad = (act_grad * up_pre * sigma * (1.0 + gate_pre * (1.0 - sigma))).astype(BF16)
    up_pgrad = (act_grad * silu_vals).astype(BF16)
    back = dot(gate_pgrad, gate_w, ((1,), (1,))) + dot(up_pgrad, up_w, ((1,), (1,)))
    back = back.astype(BF16)
    gain_part = jnp.sum(back.astype(F32) * inputs.astype(F32), axis=0, keepdims=True) / gain
    gain_part = add_from(gain_part, "dp", (1,))
    gain_part = add_from(gain_part, "tensor", (1, 2, 3))
    back, returned, gain_part = lax.optimization_barrier((back, returned, gain_part))
    back_rows = exchange(back)
    gain_part = add_from(gain_part, "dp", (2, 4, 6))

    gate_pgrad, up_pgrad, act_late = lax.optimization_barrier(
        (gate_pgrad, up_pgrad, act, back)
    )[:3]
    gate_wgrad = dot(inputs, gate_pgrad, ((0,), (0,))).astype(BF16)
    up_wgrad = dot(inputs, up_pgrad, ((0,), (0,))).astype(BF16)
    down_grad = dot(act_late, cotan, ((0,), (0,))).astype(BF16)

    halves = 2
    layer_out, gate_grad_t = pl.pallas_call(
        combine_kernel,
        grid_spec=pltpu.PrefetchScalarGridSpec(
            num_scalar_prefetch=1,
            grid=(halves,),
            in_specs=[
                whole(own, top),
                pl.BlockSpec((own, slots // halves), lambda i, q: (0, i)),
                pl.BlockSpec((3 * own, slots // halves), lambda i, q: (0, i)),
                pl.BlockSpec((slots // halves, width), lambda i, q: (i, 0)),
                pl.BlockSpec((own, width), lambda i, q: (q[0], 0)),
                whole(own, width),
            ],
            out_specs=[whole(own, width), whole(top, own)],
            scratch_shapes=[pltpu.VMEM((own, width), F32), pltpu.VMEM((own, 128), F32)],
        ),
        out_shape=[
            jax.ShapeDtypeStruct((own, width), BF16),
            jax.ShapeDtypeStruct((top, own), F32),
        ],
        compiler_params=params(),
        cost_estimate=cost(8 * own * slots * width, 2 * slots * width),
        name="combine",
    )(quarter, expert_ids, routes, weights, returned, hidden, out_grad)

    back_rows, gate_wgrad, up_wgrad, down_grad, layer_out, gate_grad_t, gain_part = (
        lax.optimization_barrier(
            (back_rows, gate_wgrad, up_wgrad, down_grad, layer_out, gate_grad_t, gain_part)
        )
    )
    gain_grad = add_from(add_from(gain_part, "dp", (8,)), "dp", (16,))[0]
    own_grad, group_grad = pl.pallas_call(
        norm_grad_kernel,
        grid_spec=pltpu.PrefetchScalarGridSpec(
            num_scalar_prefetch=1,
            grid=(halves,),
            in_specs=[
                pl.BlockSpec((own, slots // halves), lambda i, q: (0, i)),
                pl.BlockSpec((slots // halves, width), lambda i, q: (i, 0)),
                pl.BlockSpec((own, width), lambda i, q: (q[0], 0)),
                whole(1, width),
                whole(own, width),
            ],
            out_specs=[whole(own, width), pl.BlockSpec((own, width), lambda i, q: (q[0], 0))],
            scratch_shapes=[pltpu.VMEM((own, width), F32)],
        ),
        out_shape=[
            jax.ShapeDtypeStruct((own, width), BF16),
            jax.ShapeDtypeStruct(hidden.shape, BF16),
        ],
        compiler_params=params(),
        cost_estimate=cost(2 * own * slots * width, 2 * slots * width),
        name="norm_grad",
    )(quarter, routes, back_rows, hidden, gain, out_grad)
    input_grad = gather_group(own_grad, group_grad)
    return (
        layer_out,
        input_grad,
        gate_grad_t.T,
        gain_grad,
        gate_wgrad[None],
        up_wgrad[None],
        down_grad[None],
    )


def solution(mesh):
    in_specs = (
        P("dp", None),
        P(),
        P(AXES, None),
        P(AXES, None),
        P(AXES, None),
        P(AXES, None, None),
        P(AXES, None, None),
        P(AXES, None, None),
    )
    out_specs = (
        P(AXES, None),
        P("dp", None),
        P(AXES, None),
        P(),
        P(AXES, None, None),
        P(AXES, None, None),
        P(AXES, None, None),
    )
    return jax.shard_map(
        per_device, mesh=mesh, in_specs=in_specs, out_specs=out_specs, check_vma=False
    )
```

```python
import jax
import jax.numpy as jnp
from jax import lax
from jax.experimental import pallas as pl
from jax.experimental.pallas import tpu as pltpu
from jax.sharding import PartitionSpec as P

epsilon = 1e-06
AXES = ("dp", "tensor")
BF16 = jnp.bfloat16
F32 = jnp.float32
VMEM_LIMIT = 60 * 1024 * 1024


def slot_rows(ids_t, first, count, cap):
    top, tokens = ids_t.shape
    names = lax.broadcasted_iota(jnp.int32, (count, tokens), 0) + first
    named = jnp.zeros((count, tokens), F32)
    for k in range(top):
        named = named + jnp.where(ids_t[k : k + 1, :] == names, 1.0, 0.0)
    before = jnp.where(
        lax.broadcasted_iota(jnp.int32, (tokens, tokens), 0)
        < lax.broadcasted_iota(jnp.int32, (tokens, tokens), 1),
        1.0,
        0.0,
    ).astype(BF16)
    rank = jnp.dot(named.astype(BF16), before, preferred_element_type=F32)
    rank = jnp.where(named > 0.0, rank, -1.0)
    place = lax.broadcasted_iota(jnp.int32, (count, cap, tokens), 1).astype(F32)
    return jnp.where(rank[:, None, :] == place, 1.0, 0.0)


def pack_normed_kernel(quarter, ids_t, hidden, gain, out, buf, sems):
    chunks = sems.shape[0]
    rows, cap = out.shape[0] // chunks, 8
    count = rows // cap
    values = hidden[...].astype(F32)
    inverse = lax.rsqrt(jnp.mean(values * values, axis=-1, keepdims=True) + epsilon)
    normed = (values * inverse * gain[...]).astype(BF16)
    ids = ids_t[...]
    copies = []
    for chunk in range(chunks):
        chosen = slot_rows(ids, chunk * count, count, cap).reshape(rows, -1).astype(BF16)
        part = pl.ds(chunk * rows, rows)
        buf[part, :] = jnp.dot(chosen, normed, preferred_element_type=F32).astype(BF16)
        copy = pltpu.make_async_copy(buf.at[part], out.at[part], sems.at[chunk])
        copy.start()
        copies.append(copy)
    for copy in copies:
        copy.wait()


def pack_scaled_kernel(ids_t, probs_t, grad, buf):
    step = pl.program_id(0)
    rows, count, cap = buf.shape[0], buf.shape[0] // 8, 8
    ids = ids_t[...]
    top, tokens = ids.shape
    chosen = slot_rows(ids, step * count, count, cap)
    names = lax.broadcasted_iota(jnp.int32, (count, tokens), 0) + step * count
    prob = jnp.zeros((count, tokens), F32)
    for k in range(top):
        prob = prob + jnp.where(ids[k : k + 1, :] == names, probs_t[k : k + 1, :], 0.0)
    weight = jnp.sum((chosen * prob[:, None, :]).reshape(rows, tokens), axis=1, keepdims=True)
    picked = jnp.dot(
        chosen.reshape(rows, tokens).astype(BF16), grad[...], preferred_element_type=F32
    )
    buf[...] = (picked * weight).astype(BF16)


def routes_kernel(ids, probs, routes, weights):
    tokens, top = ids.shape
    slots = routes.shape[1]
    cap = 8
    experts = slots // cap
    names = lax.broadcasted_iota(jnp.int32, (tokens, experts), 1)
    named = jnp.zeros((tokens, experts), F32)
    prob = jnp.zeros((tokens, experts), F32)
    for k in range(top):
        hit = ids[:, k : k + 1] == names
        named = named + jnp.where(hit, 1.0, 0.0)
        prob = prob + jnp.where(hit, probs[:, k : k + 1], 0.0)
    before = jnp.where(
        lax.broadcasted_iota(jnp.int32, (tokens, tokens), 1)
        < lax.broadcasted_iota(jnp.int32, (tokens, tokens), 0),
        1.0,
        0.0,
    ).astype(BF16)
    rank = jnp.dot(before, named.astype(BF16), preferred_element_type=F32)
    rank = jnp.where(named > 0.0, rank, -1.0).astype(BF16)
    spread = jnp.where(
        lax.broadcasted_iota(jnp.int32, (experts, slots), 1) // cap
        == lax.broadcasted_iota(jnp.int32, (experts, slots), 0),
        1.0,
        0.0,
    ).astype(BF16)
    place = (lax.broadcasted_iota(jnp.int32, (tokens, slots), 1) % cap).astype(F32)
    chosen = jnp.where(
        jnp.dot(rank, spread, preferred_element_type=F32) == place, 1.0, 0.0
    )
    routes[...] = chosen.astype(BF16)
    left = prob
    for part in range(3):
        piece = left.astype(BF16)
        left = left - piece.astype(F32)
        weights[part * tokens : (part + 1) * tokens, :] = (
            chosen * jnp.dot(piece, spread, preferred_element_type=F32)
        ).astype(BF16)


def combine_kernel(
    quarter, ids, routes, weights, rows, hidden, grad, layer_out, gate_grad, total, found
):
    step = pl.program_id(0)
    tokens, top = ids.shape
    slots = rows.shape[0]

    @pl.when(step == 0)
    def _():
        total[...] = hidden[...].astype(F32)
        found[...] = jnp.zeros_like(found)

    parts = jnp.dot(weights[...], rows[...], preferred_element_type=F32)
    total[...] += parts[:tokens] + parts[tokens : 2 * tokens] + parts[2 * tokens :]
    dots = lax.dot_general(
        rows[...], grad[...], (((1,), (1,)), ((), ())), preferred_element_type=F32
    ).T
    mine = jnp.where(routes[...].astype(F32) > 0.0, dots, 0.0)
    expert = (lax.broadcasted_iota(jnp.int32, (tokens, slots), 1) + step * slots) // 8
    column = lax.broadcasted_iota(jnp.int32, found.shape, 1)
    sums = found[...]
    for k in range(top):
        own = jnp.where(expert == ids[:, k : k + 1], mine, 0.0)
        sums = sums + jnp.where(column == k, jnp.sum(own, axis=1, keepdims=True), 0.0)
    found[...] = sums

    @pl.when(step == pl.num_programs(0) - 1)
    def _():
        layer_out[...] = total[...].astype(BF16)
        gate_grad[...] = found[...].T[:top, :]


def norm_grad_kernel(quarter, routes, rows, hidden, gain, grad, own_grad, group_grad, total):
    step = pl.program_id(0)
    part = jnp.dot(routes[...], rows[...], preferred_element_type=F32)

    @pl.when(step == 0)
    def _():
        total[...] = part

    @pl.when(step > 0)
    def _():
        total[...] += part

    @pl.when(step == pl.num_programs(0) - 1)
    def _():
        values = hidden[...].astype(F32)
        inverse = lax.rsqrt(jnp.mean(values * values, axis=-1, keepdims=True) + epsilon)
        unit = values * inverse
        upstream = total[...] * gain[...]
        result = (
            grad[...].astype(F32)
            + inverse * (upstream - unit * jnp.mean(upstream * unit, axis=-1, keepdims=True))
        ).astype(BF16)
        own_grad[...] = result
        group_grad[...] = result


def exchange(block):
    return lax.all_to_all(block, AXES, split_axis=0, concat_axis=0, tiled=True)


def gather_group(block, whole):
    size = lax.axis_size("tensor")
    mine = lax.axis_index("tensor")
    rows = block.shape[0]
    moved = [
        (step, lax.ppermute(block, "tensor", [(i, (i + step) % size) for i in range(size)]))
        for step in (1, 3, 2)
    ]
    for step, piece in moved:
        origin = (mine + size - step) % size
        whole = lax.dynamic_update_slice_in_dim(whole, piece, origin * rows, 0)
    return whole, moved[0][1]


def add_from(value, axis, distances):
    size = lax.axis_size(axis)
    others = [
        lax.ppermute(value, axis, [(i, i ^ distance) for i in range(size)])
        for distance in distances
    ]
    for other in others:
        value = value + other
    return value


def after(value, *earlier):
    return lax.optimization_barrier((value, *earlier))[0]


def params():
    return pltpu.CompilerParams(vmem_limit_bytes=VMEM_LIMIT)


def cost(flops, moved):
    return pl.CostEstimate(flops=flops, bytes_accessed=moved, transcendentals=0)


def dot(a, b, dims):
    return lax.dot_general(a, b, (dims, ((), ())), preferred_element_type=F32)


def per_device(
    hidden, norm_gain, expert_ids, gate_probs, out_grad, gate_weight, up_weight, down_weight
):
    own, width = out_grad.shape
    top = expert_ids.shape[1]
    devices = lax.axis_size(AXES)
    cap = 8
    slots = devices * cap
    steps = 4
    quarter = lax.axis_index("tensor").astype(jnp.int32).reshape(1)
    gain = norm_gain.reshape(1, width)
    ids_t = expert_ids.T
    probs_t = gate_probs.T

    def whole(*shape):
        return pl.BlockSpec(shape, lambda *_: (0,) * len(shape))

    normed_buf = pl.pallas_call(
        pack_normed_kernel,
        grid_spec=pltpu.PrefetchScalarGridSpec(
            num_scalar_prefetch=1,
            grid=(1,),
            in_specs=[
                whole(top, own),
                pl.BlockSpec((own, width), lambda i, q: (q[0], 0)),
                whole(1, width),
            ],
            out_specs=pl.BlockSpec(memory_space=pl.ANY),
            scratch_shapes=[
                pltpu.VMEM((slots, width), BF16),
                pltpu.SemaphoreType.DMA((steps,)),
            ],
        ),
        out_shape=jax.ShapeDtypeStruct((slots, width), BF16),
        compiler_params=params(),
        cost_estimate=cost(2 * slots * own * width, 2 * slots * width),
        name="pack_normed",
    )(quarter, ids_t, hidden, gain)
    inputs = exchange(normed_buf)

    scaled_buf = pl.pallas_call(
        pack_scaled_kernel,
        grid=(steps,),
        in_specs=[whole(top, own), whole(top, own), whole(own, width)],
        out_specs=pl.BlockSpec((slots // steps, width), lambda i: (i, 0)),
        out_shape=jax.ShapeDtypeStruct((slots, width), BF16),
        compiler_params=params(),
        cost_estimate=cost(2 * slots * own * width, 2 * slots * width),
        name="pack_scaled",
    )(after(ids_t, normed_buf), probs_t, out_grad)
    cotan = exchange(after(scaled_buf, inputs))

    routes, weights = pl.pallas_call(
        routes_kernel,
        out_shape=[
            jax.ShapeDtypeStruct((own, slots), BF16),
            jax.ShapeDtypeStruct((3 * own, slots), BF16),
        ],
        compiler_params=params(),
        cost_estimate=cost(2 * 4 * own * devices * slots, 8 * own * slots),
        name="routes",
    )(after(expert_ids, normed_buf), gate_probs)

    gate_w, up_w, down_w = gate_weight[0], up_weight[0], down_weight[0]
    gate_pre = dot(inputs, gate_w, ((1,), (0,)))
    up_pre = dot(inputs, up_w, ((1,), (0,)))
    sigma = jax.nn.sigmoid(gate_pre)
    silu_vals = gate_pre * sigma
    act = (silu_vals * up_pre).astype(BF16)
    result = dot(act, down_w, ((1,), (0,))).astype(BF16)
    gate_pre, up_pre, act, cotan, result = lax.optimization_barrier(
        (gate_pre, up_pre, act, cotan, result)
    )
    returned = exchange(result)

    sigma = jax.nn.sigmoid(gate_pre)
    silu_vals = gate_pre * sigma
    act_grad = dot(cotan, down_w, ((1,), (1,)))
    gate_pgrad = (act_grad * up_pre * sigma * (1.0 + gate_pre * (1.0 - sigma))).astype(BF16)
    up_pgrad = (act_grad * silu_vals).astype(BF16)
    back = dot(gate_pgrad, gate_w, ((1,), (1,))) + dot(up_pgrad, up_w, ((1,), (1,)))
    back = lax.optimization_barrier(back.astype(BF16))
    gain_part = jnp.sum(back.astype(F32) * inputs.astype(F32), axis=0, keepdims=True) / gain
    gain_part = add_from(gain_part, "dp", (1,))
    gain_part = add_from(gain_part, "tensor", (1, 2, 3))
    back, returned, gain_part = lax.optimization_barrier((back, returned, gain_part))
    back_rows = exchange(back)
    gain_part = add_from(gain_part, "dp", (2, 4, 6))

    gate_pgrad, up_pgrad, act_late = lax.optimization_barrier(
        (gate_pgrad, up_pgrad, act, back)
    )[:3]
    gate_wgrad = dot(inputs, gate_pgrad, ((0,), (0,))).astype(BF16)
    up_wgrad = dot(inputs, up_pgrad, ((0,), (0,))).astype(BF16)
    down_grad = dot(act_late, cotan, ((0,), (0,))).astype(BF16)

    halves = 2
    layer_out, gate_grad_t = pl.pallas_call(
        combine_kernel,
        grid_spec=pltpu.PrefetchScalarGridSpec(
            num_scalar_prefetch=1,
            grid=(halves,),
            in_specs=[
                whole(own, top),
                pl.BlockSpec((own, slots // halves), lambda i, q: (0, i)),
                pl.BlockSpec((3 * own, slots // halves), lambda i, q: (0, i)),
                pl.BlockSpec((slots // halves, width), lambda i, q: (i, 0)),
                pl.BlockSpec((own, width), lambda i, q: (q[0], 0)),
                whole(own, width),
            ],
            out_specs=[whole(own, width), whole(top, own)],
            scratch_shapes=[pltpu.VMEM((own, width), F32), pltpu.VMEM((own, 128), F32)],
        ),
        out_shape=[
            jax.ShapeDtypeStruct((own, width), BF16),
            jax.ShapeDtypeStruct((top, own), F32),
        ],
        compiler_params=params(),
        cost_estimate=cost(8 * own * slots * width, 2 * slots * width),
        name="combine",
    )(quarter, expert_ids, routes, weights, returned, hidden, out_grad)

    back_rows, gate_wgrad, up_wgrad, down_grad, layer_out, gate_grad_t, gain_part = (
        lax.optimization_barrier(
            (back_rows, gate_wgrad, up_wgrad, down_grad, layer_out, gate_grad_t, gain_part)
        )
    )
    own_grad, group_grad = pl.pallas_call(
        norm_grad_kernel,
        grid_spec=pltpu.PrefetchScalarGridSpec(
            num_scalar_prefetch=1,
            grid=(halves,),
            in_specs=[
                pl.BlockSpec((own, slots // halves), lambda i, q: (0, i)),
                pl.BlockSpec((slots // halves, width), lambda i, q: (i, 0)),
                pl.BlockSpec((own, width), lambda i, q: (q[0], 0)),
                whole(1, width),
                whole(own, width),
            ],
            out_specs=[whole(own, width), pl.BlockSpec((own, width), lambda i, q: (q[0], 0))],
            scratch_shapes=[pltpu.VMEM((own, width), F32)],
        ),
        out_shape=[
            jax.ShapeDtypeStruct((own, width), BF16),
            jax.ShapeDtypeStruct(hidden.shape, BF16),
        ],
        compiler_params=params(),
        cost_estimate=cost(2 * own * slots * width, 2 * slots * width),
        name="norm_grad",
    )(quarter, routes, back_rows, hidden, gain, out_grad)
    input_grad, first = gather_group(own_grad, group_grad)
    gain_grad = add_from(after(gain_part, first), "dp", (8, 16, 24))[0]
    return (
        layer_out,
        input_grad,
        gate_grad_t.T,
        gain_grad,
        gate_wgrad[None],
        up_wgrad[None],
        down_grad[None],
    )


def solution(mesh):
    in_specs = (
        P("dp", None),
        P(),
        P(AXES, None),
        P(AXES, None),
        P(AXES, None),
        P(AXES, None, None),
        P(AXES, None, None),
        P(AXES, None, None),
    )
    out_specs = (
        P(AXES, None),
        P("dp", None),
        P(AXES, None),
        P(),
        P(AXES, None, None),
        P(AXES, None, None),
        P(AXES, None, None),
    )
    return jax.shard_map(
        per_device, mesh=mesh, in_specs=in_specs, out_specs=out_specs, check_vma=False
    )
```

```python
import jax
import jax.numpy as jnp
from jax import lax
from jax.experimental import pallas as pl
from jax.experimental.pallas import tpu as pltpu
from jax.sharding import PartitionSpec as P

epsilon = 1e-06
AXES = ("dp", "tensor")
BF16 = jnp.bfloat16
F32 = jnp.float32
VMEM_LIMIT = 60 * 1024 * 1024


def slot_rows(ids_t, first, count, cap):
    top, tokens = ids_t.shape
    names = lax.broadcasted_iota(jnp.int32, (count, tokens), 0) + first
    named = jnp.zeros((count, tokens), F32)
    for k in range(top):
        named = named + jnp.where(ids_t[k : k + 1, :] == names, 1.0, 0.0)
    before = jnp.where(
        lax.broadcasted_iota(jnp.int32, (tokens, tokens), 0)
        < lax.broadcasted_iota(jnp.int32, (tokens, tokens), 1),
        1.0,
        0.0,
    ).astype(BF16)
    rank = jnp.dot(named.astype(BF16), before, preferred_element_type=F32)
    rank = jnp.where(named > 0.0, rank, -1.0)
    place = lax.broadcasted_iota(jnp.int32, (count, cap, tokens), 1).astype(F32)
    return jnp.where(rank[:, None, :] == place, 1.0, 0.0)


def pack_normed_kernel(quarter, ids_t, hidden, gain, out, buf, sems):
    chunks = sems.shape[0]
    rows, cap = out.shape[0] // chunks, 8
    count = rows // cap
    values = hidden[...].astype(F32)
    inverse = lax.rsqrt(jnp.mean(values * values, axis=-1, keepdims=True) + epsilon)
    normed = (values * inverse * gain[...]).astype(BF16)
    ids = ids_t[...]
    copies = []
    for chunk in range(chunks):
        chosen = slot_rows(ids, chunk * count, count, cap).reshape(rows, -1).astype(BF16)
        part = pl.ds(chunk * rows, rows)
        buf[part, :] = jnp.dot(chosen, normed, preferred_element_type=F32).astype(BF16)
        copy = pltpu.make_async_copy(buf.at[part], out.at[part], sems.at[chunk])
        copy.start()
        copies.append(copy)
    for copy in copies:
        copy.wait()


def pack_scaled_kernel(ids_t, probs_t, grad, buf):
    step = pl.program_id(0)
    rows, count, cap = buf.shape[0], buf.shape[0] // 8, 8
    ids = ids_t[...]
    top, tokens = ids.shape
    chosen = slot_rows(ids, step * count, count, cap)
    names = lax.broadcasted_iota(jnp.int32, (count, tokens), 0) + step * count
    prob = jnp.zeros((count, tokens), F32)
    for k in range(top):
        prob = prob + jnp.where(ids[k : k + 1, :] == names, probs_t[k : k + 1, :], 0.0)
    weight = jnp.sum((chosen * prob[:, None, :]).reshape(rows, tokens), axis=1, keepdims=True)
    picked = jnp.dot(
        chosen.reshape(rows, tokens).astype(BF16), grad[...], preferred_element_type=F32
    )
    buf[...] = (picked * weight).astype(BF16)


def routes_kernel(ids, probs, routes, weights):
    tokens, top = ids.shape
    slots = routes.shape[1]
    cap = 8
    experts = slots // cap
    names = lax.broadcasted_iota(jnp.int32, (tokens, experts), 1)
    named = jnp.zeros((tokens, experts), F32)
    prob = jnp.zeros((tokens, experts), F32)
    for k in range(top):
        hit = ids[:, k : k + 1] == names
        named = named + jnp.where(hit, 1.0, 0.0)
        prob = prob + jnp.where(hit, probs[:, k : k + 1], 0.0)
    before = jnp.where(
        lax.broadcasted_iota(jnp.int32, (tokens, tokens), 1)
        < lax.broadcasted_iota(jnp.int32, (tokens, tokens), 0),
        1.0,
        0.0,
    ).astype(BF16)
    rank = jnp.dot(before, named.astype(BF16), preferred_element_type=F32)
    rank = jnp.where(named > 0.0, rank, -1.0).astype(BF16)
    spread = jnp.where(
        lax.broadcasted_iota(jnp.int32, (experts, slots), 1) // cap
        == lax.broadcasted_iota(jnp.int32, (experts, slots), 0),
        1.0,
        0.0,
    ).astype(BF16)
    place = (lax.broadcasted_iota(jnp.int32, (tokens, slots), 1) % cap).astype(F32)
    chosen = jnp.where(
        jnp.dot(rank, spread, preferred_element_type=F32) == place, 1.0, 0.0
    )
    routes[...] = chosen.astype(BF16)
    left = prob
    for part in range(3):
        piece = left.astype(BF16)
        left = left - piece.astype(F32)
        weights[part * tokens : (part + 1) * tokens, :] = (
            chosen * jnp.dot(piece, spread, preferred_element_type=F32)
        ).astype(BF16)


def combine_kernel(
    quarter, ids, routes, weights, rows, hidden, grad, layer_out, gate_grad, total, found
):
    step = pl.program_id(0)
    tokens, top = ids.shape
    slots = rows.shape[0]

    @pl.when(step == 0)
    def _():
        total[...] = hidden[...].astype(F32)
        found[...] = jnp.zeros_like(found)

    parts = jnp.dot(weights[...], rows[...], preferred_element_type=F32)
    total[...] += parts[:tokens] + parts[tokens : 2 * tokens] + parts[2 * tokens :]
    dots = lax.dot_general(
        rows[...], grad[...], (((1,), (1,)), ((), ())), preferred_element_type=F32
    ).T
    mine = jnp.where(routes[...].astype(F32) > 0.0, dots, 0.0)
    expert = (lax.broadcasted_iota(jnp.int32, (tokens, slots), 1) + step * slots) // 8
    column = lax.broadcasted_iota(jnp.int32, found.shape, 1)
    sums = found[...]
    for k in range(top):
        own = jnp.where(expert == ids[:, k : k + 1], mine, 0.0)
        sums = sums + jnp.where(column == k, jnp.sum(own, axis=1, keepdims=True), 0.0)
    found[...] = sums

    @pl.when(step == pl.num_programs(0) - 1)
    def _():
        layer_out[...] = total[...].astype(BF16)
        gate_grad[...] = found[...].T[:top, :]


def norm_grad_kernel(
    quarter, routes, rows, hidden, gain, grad, upper, lower, group_grad, total
):
    step = pl.program_id(0)
    part = jnp.dot(routes[...], rows[...], preferred_element_type=F32)

    @pl.when(step == 0)
    def _():
        total[...] = part

    @pl.when(step > 0)
    def _():
        total[...] += part

    @pl.when(step == pl.num_programs(0) - 1)
    def _():
        values = hidden[...].astype(F32)
        inverse = lax.rsqrt(jnp.mean(values * values, axis=-1, keepdims=True) + epsilon)
        unit = values * inverse
        upstream = total[...] * gain[...]
        result = (
            grad[...].astype(F32)
            + inverse * (upstream - unit * jnp.mean(upstream * unit, axis=-1, keepdims=True))
        ).astype(BF16)
        half = result.shape[0] // 2
        upper[...] = result[:half]
        lower[...] = result[half:]
        group_grad[...] = result


def exchange(block):
    return lax.all_to_all(block, AXES, split_axis=0, concat_axis=0, tiled=True)


def gather_group(upper, lower, whole):
    size = lax.axis_size("tensor")
    mine = lax.axis_index("tensor")
    half = upper.shape[0]
    rows = 2 * half

    def move(piece, step):
        return lax.ppermute(piece, "tensor", [(i, (i + step) % size) for i in range(size)])

    up_first, down_first = move(upper, 1), move(lower, size - 1)
    up_second, down_second = move(lower, 1), move(upper, size - 1)
    before, beyond, behind = [
        (mine + size - step) % size * rows for step in (1, 2, size - 1)
    ]
    for piece, place in (
        (up_first, before),
        (up_second, before + half),
        (down_second, behind),
        (down_first, behind + half),
        (move(up_first, 1), beyond),
        (move(down_first, size - 1), beyond + half),
    ):
        whole = lax.dynamic_update_slice_in_dim(whole, piece, place, 0)
    return whole


def add_from(value, axis, distances):
    size = lax.axis_size(axis)
    others = [
        lax.ppermute(value, axis, [(i, i ^ distance) for i in range(size)])
        for distance in distances
    ]
    for other in others:
        value = value + other
    return value


def after(value, *earlier):
    return lax.optimization_barrier((value, *earlier))[0]


def params():
    return pltpu.CompilerParams(vmem_limit_bytes=VMEM_LIMIT)


def cost(flops, moved):
    return pl.CostEstimate(flops=flops, bytes_accessed=moved, transcendentals=0)


def dot(a, b, dims):
    return lax.dot_general(a, b, (dims, ((), ())), preferred_element_type=F32)


def per_device(
    hidden, norm_gain, expert_ids, gate_probs, out_grad, gate_weight, up_weight, down_weight
):
    own, width = out_grad.shape
    top = expert_ids.shape[1]
    devices = lax.axis_size(AXES)
    cap = 8
    slots = devices * cap
    steps = 4
    quarter = lax.axis_index("tensor").astype(jnp.int32).reshape(1)
    gain = norm_gain.reshape(1, width)
    ids_t = expert_ids.T
    probs_t = gate_probs.T

    def whole(*shape):
        return pl.BlockSpec(shape, lambda *_: (0,) * len(shape))

    normed_buf = pl.pallas_call(
        pack_normed_kernel,
        grid_spec=pltpu.PrefetchScalarGridSpec(
            num_scalar_prefetch=1,
            grid=(1,),
            in_specs=[
                whole(top, own),
                pl.BlockSpec((own, width), lambda i, q: (q[0], 0)),
                whole(1, width),
            ],
            out_specs=pl.BlockSpec(memory_space=pl.ANY),
            scratch_shapes=[
                pltpu.VMEM((slots, width), BF16),
                pltpu.SemaphoreType.DMA((steps,)),
            ],
        ),
        out_shape=jax.ShapeDtypeStruct((slots, width), BF16),
        compiler_params=params(),
        cost_estimate=cost(2 * slots * own * width, 2 * slots * width),
        name="pack_normed",
    )(quarter, ids_t, hidden, gain)
    inputs = exchange(normed_buf)

    scaled_buf = pl.pallas_call(
        pack_scaled_kernel,
        grid=(steps,),
        in_specs=[whole(top, own), whole(top, own), whole(own, width)],
        out_specs=pl.BlockSpec((slots // steps, width), lambda i: (i, 0)),
        out_shape=jax.ShapeDtypeStruct((slots, width), BF16),
        compiler_params=params(),
        cost_estimate=cost(2 * slots * own * width, 2 * slots * width),
        name="pack_scaled",
    )(after(ids_t, normed_buf), probs_t, out_grad)
    cotan = exchange(after(scaled_buf, inputs))

    routes, weights = pl.pallas_call(
        routes_kernel,
        out_shape=[
            jax.ShapeDtypeStruct((own, slots), BF16),
            jax.ShapeDtypeStruct((3 * own, slots), BF16),
        ],
        compiler_params=params(),
        cost_estimate=cost(2 * 4 * own * devices * slots, 8 * own * slots),
        name="routes",
    )(after(expert_ids, normed_buf), gate_probs)

    gate_w, up_w, down_w = gate_weight[0], up_weight[0], down_weight[0]
    gate_pre = dot(inputs, gate_w, ((1,), (0,)))
    up_pre = dot(inputs, up_w, ((1,), (0,)))
    sigma = jax.nn.sigmoid(gate_pre)
    silu_vals = gate_pre * sigma
    act = (silu_vals * up_pre).astype(BF16)
    result = dot(act, down_w, ((1,), (0,))).astype(BF16)
    gate_pre, up_pre, act, cotan, result = lax.optimization_barrier(
        (gate_pre, up_pre, act, cotan, result)
    )
    returned = exchange(result)

    sigma = jax.nn.sigmoid(gate_pre)
    silu_vals = gate_pre * sigma
    act_grad = dot(cotan, down_w, ((1,), (1,)))
    gate_pgrad = (act_grad * up_pre * sigma * (1.0 + gate_pre * (1.0 - sigma))).astype(BF16)
    up_pgrad = (act_grad * silu_vals).astype(BF16)
    back = dot(gate_pgrad, gate_w, ((1,), (1,))) + dot(up_pgrad, up_w, ((1,), (1,)))
    back = lax.optimization_barrier(back.astype(BF16))
    gain_part = jnp.sum(back.astype(F32) * inputs.astype(F32), axis=0, keepdims=True) / gain
    gain_part = add_from(gain_part, "dp", (1,))
    gain_part = add_from(gain_part, "tensor", (1, 2, 3))
    back, returned, gain_part = lax.optimization_barrier((back, returned, gain_part))
    back_rows = exchange(back)
    gain_part = add_from(gain_part, "dp", (2, 4, 6))

    gate_pgrad, up_pgrad, act_late = lax.optimization_barrier(
        (gate_pgrad, up_pgrad, act, back)
    )[:3]
    gate_wgrad = dot(inputs, gate_pgrad, ((0,), (0,))).astype(BF16)
    up_wgrad = dot(inputs, up_pgrad, ((0,), (0,))).astype(BF16)
    down_grad = dot(act_late, cotan, ((0,), (0,))).astype(BF16)

    halves = 2
    layer_out, gate_grad_t = pl.pallas_call(
        combine_kernel,
        grid_spec=pltpu.PrefetchScalarGridSpec(
            num_scalar_prefetch=1,
            grid=(halves,),
            in_specs=[
                whole(own, top),
                pl.BlockSpec((own, slots // halves), lambda i, q: (0, i)),
                pl.BlockSpec((3 * own, slots // halves), lambda i, q: (0, i)),
                pl.BlockSpec((slots // halves, width), lambda i, q: (i, 0)),
                pl.BlockSpec((own, width), lambda i, q: (q[0], 0)),
                whole(own, width),
            ],
            out_specs=[whole(own, width), whole(top, own)],
            scratch_shapes=[pltpu.VMEM((own, width), F32), pltpu.VMEM((own, 128), F32)],
        ),
        out_shape=[
            jax.ShapeDtypeStruct((own, width), BF16),
            jax.ShapeDtypeStruct((top, own), F32),
        ],
        compiler_params=params(),
        cost_estimate=cost(8 * own * slots * width, 2 * slots * width),
        name="combine",
    )(quarter, expert_ids, routes, weights, returned, hidden, out_grad)

    back_rows, gate_wgrad, up_wgrad, down_grad, layer_out, gate_grad_t, gain_part = (
        lax.optimization_barrier(
            (back_rows, gate_wgrad, up_wgrad, down_grad, layer_out, gate_grad_t, gain_part)
        )
    )
    gain_grad = add_from(add_from(gain_part, "dp", (8,)), "dp", (16,))[0]
    upper, lower, group_grad = pl.pallas_call(
        norm_grad_kernel,
        grid_spec=pltpu.PrefetchScalarGridSpec(
            num_scalar_prefetch=1,
            grid=(halves,),
            in_specs=[
                pl.BlockSpec((own, slots // halves), lambda i, q: (0, i)),
                pl.BlockSpec((slots // halves, width), lambda i, q: (i, 0)),
                pl.BlockSpec((own, width), lambda i, q: (q[0], 0)),
                whole(1, width),
                whole(own, width),
            ],
            out_specs=[
                whole(own // 2, width),
                whole(own // 2, width),
                pl.BlockSpec((own, width), lambda i, q: (q[0], 0)),
            ],
            scratch_shapes=[pltpu.VMEM((own, width), F32)],
        ),
        out_shape=[
            jax.ShapeDtypeStruct((own // 2, width), BF16),
            jax.ShapeDtypeStruct((own // 2, width), BF16),
            jax.ShapeDtypeStruct(hidden.shape, BF16),
        ],
        compiler_params=params(),
        cost_estimate=cost(2 * own * slots * width, 2 * slots * width),
        name="norm_grad",
    )(quarter, routes, back_rows, hidden, gain, out_grad)
    input_grad = gather_group(upper, lower, group_grad)
    return (
        layer_out,
        input_grad,
        gate_grad_t.T,
        gain_grad,
        gate_wgrad[None],
        up_wgrad[None],
        down_grad[None],
    )


def solution(mesh):
    in_specs = (
        P("dp", None),
        P(),
        P(AXES, None),
        P(AXES, None),
        P(AXES, None),
        P(AXES, None, None),
        P(AXES, None, None),
        P(AXES, None, None),
    )
    out_specs = (
        P(AXES, None),
        P("dp", None),
        P(AXES, None),
        P(),
        P(AXES, None, None),
        P(AXES, None, None),
        P(AXES, None, None),
    )
    return jax.shard_map(
        per_device, mesh=mesh, in_specs=in_specs, out_specs=out_specs, check_vma=False
    )
```

```python
import jax
import jax.numpy as jnp
from jax import lax
from jax.experimental import pallas as pl
from jax.experimental.pallas import tpu as pltpu
from jax.sharding import PartitionSpec as P

epsilon = 1e-06
AXES = ("dp", "tensor")
BF16 = jnp.bfloat16
F32 = jnp.float32
VMEM_LIMIT = 60 * 1024 * 1024


def slot_rows(ids_t, first, count, cap):
    top, tokens = ids_t.shape
    names = lax.broadcasted_iota(jnp.int32, (count, tokens), 0) + first
    named = jnp.zeros((count, tokens), F32)
    for k in range(top):
        named = named + jnp.where(ids_t[k : k + 1, :] == names, 1.0, 0.0)
    before = jnp.where(
        lax.broadcasted_iota(jnp.int32, (tokens, tokens), 0)
        < lax.broadcasted_iota(jnp.int32, (tokens, tokens), 1),
        1.0,
        0.0,
    ).astype(BF16)
    rank = jnp.dot(named.astype(BF16), before, preferred_element_type=F32)
    rank = jnp.where(named > 0.0, rank, -1.0)
    place = lax.broadcasted_iota(jnp.int32, (count, cap, tokens), 1).astype(F32)
    return jnp.where(rank[:, None, :] == place, 1.0, 0.0)


def pack_normed_kernel(quarter, ids_t, hidden, gain, out, buf, sems):
    chunks = sems.shape[0]
    rows, cap = out.shape[0] // chunks, 8
    count = rows // cap
    values = hidden[...].astype(F32)
    inverse = lax.rsqrt(jnp.mean(values * values, axis=-1, keepdims=True) + epsilon)
    normed = (values * inverse * gain[...]).astype(BF16)
    ids = ids_t[...]
    copies = []
    for chunk in range(chunks):
        chosen = slot_rows(ids, chunk * count, count, cap).reshape(rows, -1).astype(BF16)
        part = pl.ds(chunk * rows, rows)
        buf[part, :] = jnp.dot(chosen, normed, preferred_element_type=F32).astype(BF16)
        copy = pltpu.make_async_copy(buf.at[part], out.at[part], sems.at[chunk])
        copy.start()
        copies.append(copy)
    for copy in copies:
        copy.wait()


def pack_scaled_kernel(ids_t, probs_t, grad, buf):
    step = pl.program_id(0)
    rows, count, cap = buf.shape[0], buf.shape[0] // 8, 8
    ids = ids_t[...]
    top, tokens = ids.shape
    chosen = slot_rows(ids, step * count, count, cap)
    names = lax.broadcasted_iota(jnp.int32, (count, tokens), 0) + step * count
    prob = jnp.zeros((count, tokens), F32)
    for k in range(top):
        prob = prob + jnp.where(ids[k : k + 1, :] == names, probs_t[k : k + 1, :], 0.0)
    weight = jnp.sum((chosen * prob[:, None, :]).reshape(rows, tokens), axis=1, keepdims=True)
    picked = jnp.dot(
        chosen.reshape(rows, tokens).astype(BF16), grad[...], preferred_element_type=F32
    )
    buf[...] = (picked * weight).astype(BF16)


def routes_kernel(ids, probs, routes, weights):
    tokens, top = ids.shape
    slots = routes.shape[1]
    cap = 8
    experts = slots // cap
    names = lax.broadcasted_iota(jnp.int32, (tokens, experts), 1)
    named = jnp.zeros((tokens, experts), F32)
    prob = jnp.zeros((tokens, experts), F32)
    for k in range(top):
        hit = ids[:, k : k + 1] == names
        named = named + jnp.where(hit, 1.0, 0.0)
        prob = prob + jnp.where(hit, probs[:, k : k + 1], 0.0)
    before = jnp.where(
        lax.broadcasted_iota(jnp.int32, (tokens, tokens), 1)
        < lax.broadcasted_iota(jnp.int32, (tokens, tokens), 0),
        1.0,
        0.0,
    ).astype(BF16)
    rank = jnp.dot(before, named.astype(BF16), preferred_element_type=F32)
    rank = jnp.where(named > 0.0, rank, -1.0).astype(BF16)
    spread = jnp.where(
        lax.broadcasted_iota(jnp.int32, (experts, slots), 1) // cap
        == lax.broadcasted_iota(jnp.int32, (experts, slots), 0),
        1.0,
        0.0,
    ).astype(BF16)
    place = (lax.broadcasted_iota(jnp.int32, (tokens, slots), 1) % cap).astype(F32)
    chosen = jnp.where(
        jnp.dot(rank, spread, preferred_element_type=F32) == place, 1.0, 0.0
    )
    routes[...] = chosen.astype(BF16)
    left = prob
    for part in range(3):
        piece = left.astype(BF16)
        left = left - piece.astype(F32)
        weights[part * tokens : (part + 1) * tokens, :] = (
            chosen * jnp.dot(piece, spread, preferred_element_type=F32)
        ).astype(BF16)


def combine_kernel(
    quarter, ids, routes, weights, rows, hidden, grad, layer_out, gate_grad, total, found
):
    step = pl.program_id(0)
    tokens, top = ids.shape
    slots = rows.shape[0]

    @pl.when(step == 0)
    def _():
        total[...] = hidden[...].astype(F32)
        found[...] = jnp.zeros_like(found)

    parts = jnp.dot(weights[...], rows[...], preferred_element_type=F32)
    total[...] += parts[:tokens] + parts[tokens : 2 * tokens] + parts[2 * tokens :]
    dots = lax.dot_general(
        rows[...], grad[...], (((1,), (1,)), ((), ())), preferred_element_type=F32
    ).T
    mine = jnp.where(routes[...].astype(F32) > 0.0, dots, 0.0)
    expert = (lax.broadcasted_iota(jnp.int32, (tokens, slots), 1) + step * slots) // 8
    column = lax.broadcasted_iota(jnp.int32, found.shape, 1)
    sums = found[...]
    for k in range(top):
        own = jnp.where(expert == ids[:, k : k + 1], mine, 0.0)
        sums = sums + jnp.where(column == k, jnp.sum(own, axis=1, keepdims=True), 0.0)
    found[...] = sums

    @pl.when(step == pl.num_programs(0) - 1)
    def _():
        layer_out[...] = total[...].astype(BF16)
        gate_grad[...] = found[...].T[:top, :]


def norm_grad_kernel(quarter, routes, rows, hidden, gain, grad, own_grad, group_grad, total):
    step = pl.program_id(0)
    part = jnp.dot(routes[...], rows[...], preferred_element_type=F32)

    @pl.when(step == 0)
    def _():
        total[...] = part

    @pl.when(step > 0)
    def _():
        total[...] += part

    @pl.when(step == pl.num_programs(0) - 1)
    def _():
        values = hidden[...].astype(F32)
        inverse = lax.rsqrt(jnp.mean(values * values, axis=-1, keepdims=True) + epsilon)
        unit = values * inverse
        upstream = total[...] * gain[...]
        result = (
            grad[...].astype(F32)
            + inverse * (upstream - unit * jnp.mean(upstream * unit, axis=-1, keepdims=True))
        ).astype(BF16)
        own_grad[...] = result
        group_grad[...] = result


def exchange(block):
    return lax.all_to_all(block, AXES, split_axis=0, concat_axis=0, tiled=True)


def gather_group(block, whole):
    size = lax.axis_size("tensor")
    mine = lax.axis_index("tensor")
    rows = block.shape[0]
    moved = [
        (step, lax.ppermute(block, "tensor", [(i, (i + step) % size) for i in range(size)]))
        for step in (2, 1, 3)
    ]
    for step, piece in moved:
        origin = (mine + size - step) % size
        whole = lax.dynamic_update_slice_in_dim(whole, piece, origin * rows, 0)
    return whole


def add_from(value, axis, distances):
    size = lax.axis_size(axis)
    others = [
        lax.ppermute(value, axis, [(i, i ^ distance) for i in range(size)])
        for distance in distances
    ]
    for other in others:
        value = value + other
    return value


def after(value, *earlier):
    return lax.optimization_barrier((value, *earlier))[0]


def params():
    return pltpu.CompilerParams(vmem_limit_bytes=VMEM_LIMIT)


def cost(flops, moved):
    return pl.CostEstimate(flops=flops, bytes_accessed=moved, transcendentals=0)


def dot(a, b, dims):
    return lax.dot_general(a, b, (dims, ((), ())), preferred_element_type=F32)


def per_device(
    hidden, norm_gain, expert_ids, gate_probs, out_grad, gate_weight, up_weight, down_weight
):
    own, width = out_grad.shape
    top = expert_ids.shape[1]
    devices = lax.axis_size(AXES)
    cap = 8
    slots = devices * cap
    steps = 4
    quarter = lax.axis_index("tensor").astype(jnp.int32).reshape(1)
    gain = norm_gain.reshape(1, width)
    ids_t = expert_ids.T
    probs_t = gate_probs.T

    def whole(*shape):
        return pl.BlockSpec(shape, lambda *_: (0,) * len(shape))

    normed_buf = pl.pallas_call(
        pack_normed_kernel,
        grid_spec=pltpu.PrefetchScalarGridSpec(
            num_scalar_prefetch=1,
            grid=(1,),
            in_specs=[
                whole(top, own),
                pl.BlockSpec((own, width), lambda i, q: (q[0], 0)),
                whole(1, width),
            ],
            out_specs=pl.BlockSpec(memory_space=pl.ANY),
            scratch_shapes=[
                pltpu.VMEM((slots, width), BF16),
                pltpu.SemaphoreType.DMA((steps,)),
            ],
        ),
        out_shape=jax.ShapeDtypeStruct((slots, width), BF16),
        compiler_params=params(),
        cost_estimate=cost(2 * slots * own * width, 2 * slots * width),
        name="pack_normed",
    )(quarter, ids_t, hidden, gain)
    inputs = exchange(normed_buf)

    scaled_buf = pl.pallas_call(
        pack_scaled_kernel,
        grid=(steps,),
        in_specs=[whole(top, own), whole(top, own), whole(own, width)],
        out_specs=pl.BlockSpec((slots // steps, width), lambda i: (i, 0)),
        out_shape=jax.ShapeDtypeStruct((slots, width), BF16),
        compiler_params=params(),
        cost_estimate=cost(2 * slots * own * width, 2 * slots * width),
        name="pack_scaled",
    )(after(ids_t, normed_buf), probs_t, out_grad)
    cotan = exchange(after(scaled_buf, inputs))

    routes, weights = pl.pallas_call(
        routes_kernel,
        out_shape=[
            jax.ShapeDtypeStruct((own, slots), BF16),
            jax.ShapeDtypeStruct((3 * own, slots), BF16),
        ],
        compiler_params=params(),
        cost_estimate=cost(2 * 4 * own * devices * slots, 8 * own * slots),
        name="routes",
    )(after(expert_ids, normed_buf), gate_probs)

    gate_w, up_w, down_w = gate_weight[0], up_weight[0], down_weight[0]
    gate_pre = dot(inputs, gate_w, ((1,), (0,)))
    up_pre = dot(inputs, up_w, ((1,), (0,)))
    sigma = jax.nn.sigmoid(gate_pre)
    silu_vals = gate_pre * sigma
    act = (silu_vals * up_pre).astype(BF16)
    result = dot(act, down_w, ((1,), (0,))).astype(BF16)
    gate_pre, up_pre, act, cotan, result = lax.optimization_barrier(
        (gate_pre, up_pre, act, cotan, result)
    )
    returned = exchange(result)

    sigma = jax.nn.sigmoid(gate_pre)
    silu_vals = gate_pre * sigma
    act_grad = dot(cotan, down_w, ((1,), (1,)))
    gate_pgrad = (act_grad * up_pre * sigma * (1.0 + gate_pre * (1.0 - sigma))).astype(BF16)
    up_pgrad = (act_grad * silu_vals).astype(BF16)
    back = dot(gate_pgrad, gate_w, ((1,), (1,))) + dot(up_pgrad, up_w, ((1,), (1,)))
    back = lax.optimization_barrier(back.astype(BF16))
    gain_part = jnp.sum(back.astype(F32) * inputs.astype(F32), axis=0, keepdims=True) / gain
    gain_part = add_from(gain_part, "dp", (1,))
    gain_part = add_from(gain_part, "tensor", (1, 2, 3))
    back, returned, gain_part = lax.optimization_barrier((back, returned, gain_part))
    back_rows = exchange(back)
    gain_part = add_from(gain_part, "dp", (2, 4, 6))

    gate_pgrad, up_pgrad, act_late = lax.optimization_barrier(
        (gate_pgrad, up_pgrad, act, back)
    )[:3]
    gate_wgrad = dot(inputs, gate_pgrad, ((0,), (0,))).astype(BF16)
    up_wgrad = dot(inputs, up_pgrad, ((0,), (0,))).astype(BF16)
    down_grad = dot(act_late, cotan, ((0,), (0,))).astype(BF16)

    halves = 2
    layer_out, gate_grad_t = pl.pallas_call(
        combine_kernel,
        grid_spec=pltpu.PrefetchScalarGridSpec(
            num_scalar_prefetch=1,
            grid=(halves,),
            in_specs=[
                whole(own, top),
                pl.BlockSpec((own, slots // halves), lambda i, q: (0, i)),
                pl.BlockSpec((3 * own, slots // halves), lambda i, q: (0, i)),
                pl.BlockSpec((slots // halves, width), lambda i, q: (i, 0)),
                pl.BlockSpec((own, width), lambda i, q: (q[0], 0)),
                whole(own, width),
            ],
            out_specs=[whole(own, width), whole(top, own)],
            scratch_shapes=[pltpu.VMEM((own, width), F32), pltpu.VMEM((own, 128), F32)],
        ),
        out_shape=[
            jax.ShapeDtypeStruct((own, width), BF16),
            jax.ShapeDtypeStruct((top, own), F32),
        ],
        compiler_params=params(),
        cost_estimate=cost(8 * own * slots * width, 2 * slots * width),
        name="combine",
    )(quarter, expert_ids, routes, weights, returned, hidden, out_grad)

    back_rows, gate_wgrad, up_wgrad, down_grad, layer_out, gate_grad_t, gain_part = (
        lax.optimization_barrier(
            (back_rows, gate_wgrad, up_wgrad, down_grad, layer_out, gate_grad_t, gain_part)
        )
    )
    gain_grad = add_from(add_from(gain_part, "dp", (8,)), "dp", (16,))[0]
    own_grad, group_grad = pl.pallas_call(
        norm_grad_kernel,
        grid_spec=pltpu.PrefetchScalarGridSpec(
            num_scalar_prefetch=1,
            grid=(halves,),
            in_specs=[
                pl.BlockSpec((own, slots // halves), lambda i, q: (0, i)),
                pl.BlockSpec((slots // halves, width), lambda i, q: (i, 0)),
                pl.BlockSpec((own, width), lambda i, q: (q[0], 0)),
                whole(1, width),
                whole(own, width),
            ],
            out_specs=[whole(own, width), pl.BlockSpec((own, width), lambda i, q: (q[0], 0))],
            scratch_shapes=[pltpu.VMEM((own, width), F32)],
        ),
        out_shape=[
            jax.ShapeDtypeStruct((own, width), BF16),
            jax.ShapeDtypeStruct(hidden.shape, BF16),
        ],
        compiler_params=params(),
        cost_estimate=cost(2 * own * slots * width, 2 * slots * width),
        name="norm_grad",
    )(quarter, routes, back_rows, hidden, gain, out_grad)
    input_grad = gather_group(own_grad, group_grad)
    return (
        layer_out,
        input_grad,
        gate_grad_t.T,
        gain_grad,
        gate_wgrad[None],
        up_wgrad[None],
        down_grad[None],
    )


def solution(mesh):
    in_specs = (
        P("dp", None),
        P(),
        P(AXES, None),
        P(AXES, None),
        P(AXES, None),
        P(AXES, None, None),
        P(AXES, None, None),
        P(AXES, None, None),
    )
    out_specs = (
        P(AXES, None),
        P("dp", None),
        P(AXES, None),
        P(),
        P(AXES, None, None),
        P(AXES, None, None),
        P(AXES, None, None),
    )
    return jax.shard_map(
        per_device, mesh=mesh, in_specs=in_specs, out_specs=out_specs, check_vma=False
    )
```

```python
import jax
import jax.numpy as jnp
from jax import lax
from jax.experimental import pallas as pl
from jax.experimental.pallas import tpu as pltpu
from jax.sharding import PartitionSpec as P

epsilon = 1e-06
AXES = ("dp", "tensor")
BF16 = jnp.bfloat16
F32 = jnp.float32
VMEM_LIMIT = 60 * 1024 * 1024


def slot_rows(ids_t, first, count, cap):
    top, tokens = ids_t.shape
    names = lax.broadcasted_iota(jnp.int32, (count, tokens), 0) + first
    named = jnp.zeros((count, tokens), F32)
    for k in range(top):
        named = named + jnp.where(ids_t[k : k + 1, :] == names, 1.0, 0.0)
    before = jnp.where(
        lax.broadcasted_iota(jnp.int32, (tokens, tokens), 0)
        < lax.broadcasted_iota(jnp.int32, (tokens, tokens), 1),
        1.0,
        0.0,
    ).astype(BF16)
    rank = jnp.dot(named.astype(BF16), before, preferred_element_type=F32)
    rank = jnp.where(named > 0.0, rank, -1.0)
    place = lax.broadcasted_iota(jnp.int32, (count, cap, tokens), 1).astype(F32)
    return jnp.where(rank[:, None, :] == place, 1.0, 0.0)


def pack_normed_kernel(quarter, ids_t, hidden, gain, out, buf, sems):
    chunks = sems.shape[0]
    rows, cap = out.shape[0] // chunks, 8
    count = rows // cap
    values = hidden[...].astype(F32)
    inverse = lax.rsqrt(jnp.mean(values * values, axis=-1, keepdims=True) + epsilon)
    normed = (values * inverse * gain[...]).astype(BF16)
    ids = ids_t[...]
    copies = []
    for chunk in range(chunks):
        chosen = slot_rows(ids, chunk * count, count, cap).reshape(rows, -1).astype(BF16)
        part = pl.ds(chunk * rows, rows)
        buf[part, :] = jnp.dot(chosen, normed, preferred_element_type=F32).astype(BF16)
        copy = pltpu.make_async_copy(buf.at[part], out.at[part], sems.at[chunk])
        copy.start()
        copies.append(copy)
    for copy in copies:
        copy.wait()


def pack_scaled_kernel(ids_t, probs_t, grad, buf):
    step = pl.program_id(0)
    rows, count, cap = buf.shape[0], buf.shape[0] // 8, 8
    ids = ids_t[...]
    top, tokens = ids.shape
    chosen = slot_rows(ids, step * count, count, cap)
    names = lax.broadcasted_iota(jnp.int32, (count, tokens), 0) + step * count
    prob = jnp.zeros((count, tokens), F32)
    for k in range(top):
        prob = prob + jnp.where(ids[k : k + 1, :] == names, probs_t[k : k + 1, :], 0.0)
    weight = jnp.sum((chosen * prob[:, None, :]).reshape(rows, tokens), axis=1, keepdims=True)
    picked = jnp.dot(
        chosen.reshape(rows, tokens).astype(BF16), grad[...], preferred_element_type=F32
    )
    buf[...] = (picked * weight).astype(BF16)


def routes_kernel(ids, probs, routes, weights):
    tokens, top = ids.shape
    slots = routes.shape[1]
    cap = 8
    experts = slots // cap
    names = lax.broadcasted_iota(jnp.int32, (tokens, experts), 1)
    named = jnp.zeros((tokens, experts), F32)
    prob = jnp.zeros((tokens, experts), F32)
    for k in range(top):
        hit = ids[:, k : k + 1] == names
        named = named + jnp.where(hit, 1.0, 0.0)
        prob = prob + jnp.where(hit, probs[:, k : k + 1], 0.0)
    before = jnp.where(
        lax.broadcasted_iota(jnp.int32, (tokens, tokens), 1)
        < lax.broadcasted_iota(jnp.int32, (tokens, tokens), 0),
        1.0,
        0.0,
    ).astype(BF16)
    rank = jnp.dot(before, named.astype(BF16), preferred_element_type=F32)
    rank = jnp.where(named > 0.0, rank, -1.0).astype(BF16)
    spread = jnp.where(
        lax.broadcasted_iota(jnp.int32, (experts, slots), 1) // cap
        == lax.broadcasted_iota(jnp.int32, (experts, slots), 0),
        1.0,
        0.0,
    ).astype(BF16)
    place = (lax.broadcasted_iota(jnp.int32, (tokens, slots), 1) % cap).astype(F32)
    chosen = jnp.where(
        jnp.dot(rank, spread, preferred_element_type=F32) == place, 1.0, 0.0
    )
    routes[...] = chosen.astype(BF16)
    left = prob
    for part in range(3):
        piece = left.astype(BF16)
        left = left - piece.astype(F32)
        weights[part * tokens : (part + 1) * tokens, :] = (
            chosen * jnp.dot(piece, spread, preferred_element_type=F32)
        ).astype(BF16)


def combine_kernel(
    quarter, ids, routes, weights, rows, hidden, grad, layer_out, gate_grad, total, found
):
    step = pl.program_id(0)
    tokens, top = ids.shape
    slots = rows.shape[0]

    @pl.when(step == 0)
    def _():
        total[...] = hidden[...].astype(F32)
        found[...] = jnp.zeros_like(found)

    parts = jnp.dot(weights[...], rows[...], preferred_element_type=F32)
    total[...] += parts[:tokens] + parts[tokens : 2 * tokens] + parts[2 * tokens :]
    dots = lax.dot_general(
        rows[...], grad[...], (((1,), (1,)), ((), ())), preferred_element_type=F32
    ).T
    mine = jnp.where(routes[...].astype(F32) > 0.0, dots, 0.0)
    expert = (lax.broadcasted_iota(jnp.int32, (tokens, slots), 1) + step * slots) // 8
    column = lax.broadcasted_iota(jnp.int32, found.shape, 1)
    sums = found[...]
    for k in range(top):
        own = jnp.where(expert == ids[:, k : k + 1], mine, 0.0)
        sums = sums + jnp.where(column == k, jnp.sum(own, axis=1, keepdims=True), 0.0)
    found[...] = sums

    @pl.when(step == pl.num_programs(0) - 1)
    def _():
        layer_out[...] = total[...].astype(BF16)
        gate_grad[...] = found[...].T[:top, :]


def norm_grad_kernel(quarter, routes, rows, hidden, gain, grad, own_grad, group_grad, total):
    step = pl.program_id(0)
    part = jnp.dot(routes[...], rows[...], preferred_element_type=F32)

    @pl.when(step == 0)
    def _():
        total[...] = part

    @pl.when(step > 0)
    def _():
        total[...] += part

    @pl.when(step == pl.num_programs(0) - 1)
    def _():
        values = hidden[...].astype(F32)
        inverse = lax.rsqrt(jnp.mean(values * values, axis=-1, keepdims=True) + epsilon)
        unit = values * inverse
        upstream = total[...] * gain[...]
        result = (
            grad[...].astype(F32)
            + inverse * (upstream - unit * jnp.mean(upstream * unit, axis=-1, keepdims=True))
        ).astype(BF16)
        own_grad[...] = result
        group_grad[...] = result


def exchange(block):
    return lax.all_to_all(block, AXES, split_axis=0, concat_axis=0, tiled=True)


def gather_group(block, whole):
    size = lax.axis_size("tensor")
    mine = lax.axis_index("tensor")
    rows = block.shape[0]
    moved = [
        (step, lax.ppermute(block, "tensor", [(i, (i + step) % size) for i in range(size)]))
        for step in (2, 1, 3)
    ]
    for step, piece in moved:
        origin = (mine + size - step) % size
        whole = lax.dynamic_update_slice_in_dim(whole, piece, origin * rows, 0)
    return whole


def add_from(value, axis, distances):
    size = lax.axis_size(axis)
    others = [
        lax.ppermute(value, axis, [(i, i ^ distance) for i in range(size)])
        for distance in distances
    ]
    for other in others:
        value = value + other
    return value


def after(value, *earlier):
    return lax.optimization_barrier((value, *earlier))[0]


def params():
    return pltpu.CompilerParams(vmem_limit_bytes=VMEM_LIMIT)


def cost(flops, moved):
    return pl.CostEstimate(flops=flops, bytes_accessed=moved, transcendentals=0)


def dot(a, b, dims):
    return lax.dot_general(a, b, (dims, ((), ())), preferred_element_type=F32)


def per_device(
    hidden, norm_gain, expert_ids, gate_probs, out_grad, gate_weight, up_weight, down_weight
):
    own, width = out_grad.shape
    top = expert_ids.shape[1]
    devices = lax.axis_size(AXES)
    cap = 8
    slots = devices * cap
    steps = 4
    quarter = lax.axis_index("tensor").astype(jnp.int32).reshape(1)
    gain = norm_gain.reshape(1, width)
    ids_t = expert_ids.T
    probs_t = gate_probs.T

    def whole(*shape):
        return pl.BlockSpec(shape, lambda *_: (0,) * len(shape))

    normed_buf = pl.pallas_call(
        pack_normed_kernel,
        grid_spec=pltpu.PrefetchScalarGridSpec(
            num_scalar_prefetch=1,
            grid=(1,),
            in_specs=[
                whole(top, own),
                pl.BlockSpec((own, width), lambda i, q: (q[0], 0)),
                whole(1, width),
            ],
            out_specs=pl.BlockSpec(memory_space=pl.ANY),
            scratch_shapes=[
                pltpu.VMEM((slots, width), BF16),
                pltpu.SemaphoreType.DMA((steps,)),
            ],
        ),
        out_shape=jax.ShapeDtypeStruct((slots, width), BF16),
        compiler_params=params(),
        cost_estimate=cost(2 * slots * own * width, 2 * slots * width),
        name="pack_normed",
    )(quarter, ids_t, hidden, gain)
    inputs = exchange(normed_buf)

    scaled_buf = pl.pallas_call(
        pack_scaled_kernel,
        grid=(steps,),
        in_specs=[whole(top, own), whole(top, own), whole(own, width)],
        out_specs=pl.BlockSpec((slots // steps, width), lambda i: (i, 0)),
        out_shape=jax.ShapeDtypeStruct((slots, width), BF16),
        compiler_params=params(),
        cost_estimate=cost(2 * slots * own * width, 2 * slots * width),
        name="pack_scaled",
    )(after(ids_t, normed_buf), probs_t, out_grad)
    cotan = exchange(after(scaled_buf, inputs))

    routes, weights = pl.pallas_call(
        routes_kernel,
        out_shape=[
            jax.ShapeDtypeStruct((own, slots), BF16),
            jax.ShapeDtypeStruct((3 * own, slots), BF16),
        ],
        compiler_params=params(),
        cost_estimate=cost(2 * 4 * own * devices * slots, 8 * own * slots),
        name="routes",
    )(after(expert_ids, normed_buf), gate_probs)

    gate_w, up_w, down_w = gate_weight[0], up_weight[0], down_weight[0]
    gate_pre = dot(inputs, gate_w, ((1,), (0,)))
    up_pre = dot(inputs, up_w, ((1,), (0,)))
    sigma = jax.nn.sigmoid(gate_pre)
    silu_vals = gate_pre * sigma
    act = (silu_vals * up_pre).astype(BF16)
    result = dot(act, down_w, ((1,), (0,))).astype(BF16)
    gate_pre, up_pre, act, cotan, result = lax.optimization_barrier(
        (gate_pre, up_pre, act, cotan, result)
    )
    returned = exchange(result)

    sigma = jax.nn.sigmoid(gate_pre)
    silu_vals = gate_pre * sigma
    act_grad = dot(cotan, down_w, ((1,), (1,)))
    gate_pgrad = (act_grad * up_pre * sigma * (1.0 + gate_pre * (1.0 - sigma))).astype(BF16)
    up_pgrad = (act_grad * silu_vals).astype(BF16)
    back = dot(gate_pgrad, gate_w, ((1,), (1,))) + dot(up_pgrad, up_w, ((1,), (1,)))
    back = lax.optimization_barrier(back.astype(BF16))
    gain_part = jnp.sum(back.astype(F32) * inputs.astype(F32), axis=0, keepdims=True) / gain
    gain_part = add_from(gain_part, "dp", (1,))
    gain_part = add_from(gain_part, "tensor", (1, 2, 3))
    back, returned, gain_part = lax.optimization_barrier((back, returned, gain_part))
    back_rows = exchange(back)
    gain_part = add_from(add_from(gain_part, "dp", (2, 4, 6)), "dp", (8,))

    gate_pgrad, up_pgrad, act_late = lax.optimization_barrier(
        (gate_pgrad, up_pgrad, act, back)
    )[:3]
    gate_wgrad = dot(inputs, gate_pgrad, ((0,), (0,))).astype(BF16)
    up_wgrad = dot(inputs, up_pgrad, ((0,), (0,))).astype(BF16)
    down_grad = dot(act_late, cotan, ((0,), (0,))).astype(BF16)

    halves = 2
    layer_out, gate_grad_t = pl.pallas_call(
        combine_kernel,
        grid_spec=pltpu.PrefetchScalarGridSpec(
            num_scalar_prefetch=1,
            grid=(halves,),
            in_specs=[
                whole(own, top),
                pl.BlockSpec((own, slots // halves), lambda i, q: (0, i)),
                pl.BlockSpec((3 * own, slots // halves), lambda i, q: (0, i)),
                pl.BlockSpec((slots // halves, width), lambda i, q: (i, 0)),
                pl.BlockSpec((own, width), lambda i, q: (q[0], 0)),
                whole(own, width),
            ],
            out_specs=[whole(own, width), whole(top, own)],
            scratch_shapes=[pltpu.VMEM((own, width), F32), pltpu.VMEM((own, 128), F32)],
        ),
        out_shape=[
            jax.ShapeDtypeStruct((own, width), BF16),
            jax.ShapeDtypeStruct((top, own), F32),
        ],
        compiler_params=params(),
        cost_estimate=cost(8 * own * slots * width, 2 * slots * width),
        name="combine",
    )(quarter, expert_ids, routes, weights, returned, hidden, out_grad)

    back_rows, gate_wgrad, up_wgrad, down_grad, layer_out, gate_grad_t, gain_part = (
        lax.optimization_barrier(
            (back_rows, gate_wgrad, up_wgrad, down_grad, layer_out, gate_grad_t, gain_part)
        )
    )
    gain_grad = add_from(gain_part, "dp", (16,))[0]
    own_grad, group_grad = pl.pallas_call(
        norm_grad_kernel,
        grid_spec=pltpu.PrefetchScalarGridSpec(
            num_scalar_prefetch=1,
            grid=(halves,),
            in_specs=[
                pl.BlockSpec((own, slots // halves), lambda i, q: (0, i)),
                pl.BlockSpec((slots // halves, width), lambda i, q: (i, 0)),
                pl.BlockSpec((own, width), lambda i, q: (q[0], 0)),
                whole(1, width),
                whole(own, width),
            ],
            out_specs=[whole(own, width), pl.BlockSpec((own, width), lambda i, q: (q[0], 0))],
            scratch_shapes=[pltpu.VMEM((own, width), F32)],
        ),
        out_shape=[
            jax.ShapeDtypeStruct((own, width), BF16),
            jax.ShapeDtypeStruct(hidden.shape, BF16),
        ],
        compiler_params=params(),
        cost_estimate=cost(2 * own * slots * width, 2 * slots * width),
        name="norm_grad",
    )(quarter, routes, back_rows, hidden, gain, out_grad)
    input_grad = gather_group(own_grad, group_grad)
    return (
        layer_out,
        input_grad,
        gate_grad_t.T,
        gain_grad,
        gate_wgrad[None],
        up_wgrad[None],
        down_grad[None],
    )


def solution(mesh):
    in_specs = (
        P("dp", None),
        P(),
        P(AXES, None),
        P(AXES, None),
        P(AXES, None),
        P(AXES, None, None),
        P(AXES, None, None),
        P(AXES, None, None),
    )
    out_specs = (
        P(AXES, None),
        P("dp", None),
        P(AXES, None),
        P(),
        P(AXES, None, None),
        P(AXES, None, None),
        P(AXES, None, None),
    )
    return jax.shard_map(
        per_device, mesh=mesh, in_specs=in_specs, out_specs=out_specs, check_vma=False
    )
```
